128 devices in a mesh: row: 8 (over z, x_hi), col: 16 (over y, x_lo, core).
Axes of the slice: x: 4 (x_hi: 2, x_lo: 2; x = x_hi * 2 + x_lo), y: 4, z: 4, core: 2. Of those that a mesh axis runs over, the one named last changes fastest.
Arguments:
- inputs: bfloat16 [1024, 12288], P(('row', 'col')), may hold values from -24 to 24
- cotangent: bfloat16 [1024, 12288], P('row', 'col'), may hold values from -6 to 6
- w_in: bfloat16 [12288, 24576], P('col', 'row'), may hold values from -0.109375 to 0.109375
- w_out: bfloat16 [24576, 12288], P('row', 'col'), may hold values from -0.078125 to 0.078125
- mask_in: int32 [192, 384], P('col', 'row'), may hold values 0 or 1
- mask_out: int32 [384, 192], P('row', 'col'), may hold values 0 or 1
Outputs:
- output: bfloat16 [1024, 12288], P('row', 'col')
- input_grad: bfloat16 [1024, 12288], P('row', 'col')
- w_in_grad: bfloat16 [12288, 24576], P('col', 'row')
- w_out_grad: bfloat16 [24576, 12288], P('row', 'col')
The draws below stay inside these ranges and needn't reach their ends.
All inputs are finite; a program needn't handle non-finite values. No bound on the sum of `mask_in` or of `mask_out` on one device may be relied on, other than what follows from the above.
Results may differ from the reference program's by a relative error of at most 0.0051.
Values may be sent and summed in bfloat16 or wider, within the bound.
A program may use at most 192 MiB of HBM per device.

```python
import jax
import jax.numpy as jnp
from jax import lax

D = 12288
FF = 24576
BLOCK = 64
TOKENS = 1024


def place_ends(entries, own_key, least, top_value):
    extent = entries.shape
    place = [jax.random.randint(jax.random.fold_in(own_key, axis), (), 0, extent[axis]) for axis in range(len(extent))]
    entries = entries.at[tuple(place)].set(least)
    longest = extent.index(max(extent))
    place[longest] = (place[longest] + 1) % extent[longest]
    return entries.at[tuple(place)].set(top_value)


def strengthened(values, rng, source, target, shards_of, factor):
    owner, partner = [(jnp.arange(values.shape[position]) // (values.shape[position] // shards_of)).reshape([-1 if axis == position else 1 for axis in range(values.ndim)]) for position in (source, target)]
    chosen = jax.random.permutation(rng, shards_of)[partner]
    strong = (owner == chosen) | (owner == (partner + shards_of // 2) % shards_of)
    return jnp.where(strong, factor * values, values)


def levels(stream_key, dims, split, least, largest):
    loudness, own = 1.0, jax.random.fold_in(stream_key, 6)
    for position, parts in split:
        draws = jnp.exp(jax.random.uniform(jax.random.fold_in(own, position), (parts,), jnp.float32, least / len(split), largest / len(split)))
        loudness = loudness * jnp.repeat(draws, dims[position] // parts).reshape([-1 if axis == position else 1 for axis in range(len(dims))])
    return loudness


def gaussian(key, shape, scale, bound, split=(), kind=jnp.bfloat16):
    factor_of = levels(key, shape, split, -0.22, 0.18) if split else 1.0
    array = jax.random.normal(key, shape, jnp.float32) * scale * factor_of
    return jnp.minimum(jnp.maximum(array, -bound), bound).astype(kind)


def heavy_noise(rng, extent, deviation, most, split, heavy, kind=jnp.bfloat16):
    result = deviation * jax.random.normal(rng, extent, jnp.float32)
    if split:
        result = result * levels(rng, extent, split, -0.22, 0.18)
    return jnp.clip(strengthened(result, jax.random.fold_in(rng, 3), *heavy), -most, most).astype(kind)


def setup_inputs(seed: int = 0) -> dict:
    splits = jax.random.split(jax.random.key(seed), 7)
    inputs = heavy_noise(splits[0], (TOKENS, D), 1.0, 24.0, ((0, 128),), (1, 0, 128, 5.5))
    cotangent = heavy_noise(splits[1], (TOKENS, D), 1.0, 6.0, ((0, 8), (1, 16)), (1, 0, 16, 2.0))
    w_in = gaussian(splits[2], (D, FF), (D // 4) ** -0.5, 0.109375, ((0, 16), (1, 8)))
    w_out = gaussian(splits[3], (FF, D), (FF // 4) ** -0.5, 0.078125, ((0, 8), (1, 16)))
    mask_in = place_ends((jax.random.randint(splits[4], (D // BLOCK, FF // BLOCK), 0, 4) < 1).astype(jnp.int32), jax.random.fold_in(splits[4], 1), 0, 1)
    mask_out = place_ends((jax.random.randint(splits[5], (FF // BLOCK, D // BLOCK), 0, 4) < 1).astype(jnp.int32), jax.random.fold_in(splits[5], 1), 0, 1)
    return {"inputs": inputs, "cotangent": cotangent, "w_in": w_in, "w_out": w_out, "mask_in": mask_in, "mask_out": mask_out}


def masked(weight, blocks):
    block_rows, block_cols = blocks.shape
    shaped = weight.reshape(block_rows, weight.shape[0] // block_rows, block_cols, weight.shape[1] // block_cols)
    return (shaped * blocks.astype(weight.dtype)[:, None, :, None]).reshape(weight.shape)

def gelu_tanh(values):
    return jax.nn.gelu(values, approximate=True)

def gelu_back(hidden, act_grad):
    unused, pullback = jax.vjp(gelu_tanh, hidden)
    return pullback(act_grad)[0]

def reference(inputs, cotangent, w_in, w_out, mask_in, mask_out):
    first = masked(w_in, mask_in)
    second = masked(w_out, mask_out)
    hidden = jnp.dot(inputs, first, preferred_element_type=jnp.float32)
    activated = gelu_tanh(hidden).astype(jnp.bfloat16)
    output = jnp.dot(activated, second, preferred_element_type=jnp.float32).astype(jnp.bfloat16)
    act_grad = lax.dot_general(cotangent, second, (((1,), (1,)), ((), ())), preferred_element_type=jnp.float32)
    hidden_grad = gelu_back(hidden, act_grad).astype(jnp.bfloat16)
    input_grad = lax.dot_general(hidden_grad, first, (((1,), (1,)), ((), ())), preferred_element_type=jnp.float32).astype(jnp.bfloat16)
    in_product = lax.dot_general(inputs, hidden_grad, (((0,), (0,)), ((), ())), preferred_element_type=jnp.float32)
    w_in_grad = masked(in_product, mask_in).astype(jnp.bfloat16)
    out_product = lax.dot_general(activated, cotangent, (((0,), (0,)), ((), ())), preferred_element_type=jnp.float32)
    w_out_grad = masked(out_product, mask_out).astype(jnp.bfloat16)
    return (output, input_grad, w_in_grad, w_out_grad)
```

```python
import functools

import jax
import jax.numpy as jnp
from jax import lax
from jax.experimental import pallas as pl
from jax.experimental.pallas import tpu as pltpu
from jax.sharding import PartitionSpec as P

MESH = pl.DeviceIdType.MESH
F32 = jnp.float32
BF16 = jnp.bfloat16

GROUP = 128
GROUPS = 8
FEAT = 768
HALF = 1536
XW = 896
YW = HALF - XW
TILE = 256


def flip(position, by):
    return (position % 2 + by % 2) % 2 + 2 * ((position // 2 + by // 2) % 2)


def one_hot(shape, along, shift, offset):
    wide = lax.broadcasted_iota(jnp.int32, shape, along)
    other = lax.broadcasted_iota(jnp.int32, shape, 1 - along)
    return (lax.shift_right_logical(wide, shift) + offset == other).astype(F32).astype(BF16)


def gelu_parts(hidden, act_grad):
    c = 0.7978845608028654
    square = hidden * hidden
    inner = jnp.tanh(c * hidden * (1.0 + 0.044715 * square))
    cdf = 0.5 * (1.0 + inner)
    slope = cdf + 0.5 * hidden * (1.0 - inner * inner) * (c * (1.0 + 0.134145 * square))
    return hidden * cdf, act_grad * slope


def pipeline(
    inputs_ref, cot_ref, w_in_ref, w_out_ref, mask_in_ref, mask_out_ref,
    out_ref, ig_ref, xg_out, ahg_out,
    w1, w2, s1, s2, m_in, m_out, a2a_send, a2a_recv, xg, part, rs1_send,
    r1x, r1y, sum_x, sum_y, rs2_sx, rs2_sy, r2y, r2x, ahg, prod, sib_send, sib_recv,
    row_send, row_recv, row_own, hop_send, hop_recv,
    load_sem, wsend_sem, wrecv_sem, a_ssem, a_rsem, g_ssem, g_rsem, f_ssem, f_rsem,
    rs1_ss, rs1_rs, rs2_ss, rs2_rs, ag1_ss, ag1_rs, ag2_ss, ag2_rs,
    sib_ss, sib_rs, row_ss, row_rs, keep_sem, give_ss, give_rs, hop_ss, hop_rs,
):
    row, col = lax.axis_index("row"), lax.axis_index("col")
    z, xh = row // 2, row % 2
    chip, core = col // 2, col % 2
    y, x = chip // 2, chip % 2

    sibling = (row, chip * 2 + 1 - core)
    x_mate = (row, (y * 2 + 1 - x) * 2 + core)
    y_mate = [(row, (flip(y, d) * 2 + x) * 2 + core) for d in (1, 2, 3)]
    hop_mate = (z * 2 + 1 - xh, col)
    z_mate = [(flip(z, d) * 2 + xh, col) for d in (1, 2, 3)]
    col_mate = [(row, (col + d) % 16) for d in range(1, 16)]

    def remote(source, target, send, recv, device):
        return pltpu.make_async_remote_copy(
            src_ref=source, dst_ref=target, send_sem=send, recv_sem=recv,
            device_id=device, device_id_type=MESH,
        )

    loads = [
        pltpu.make_async_copy(w_in_ref.at[:, pl.ds(pl.multiple_of((1 - core) * HALF, HALF), HALF)], s1, load_sem.at[0]),
        pltpu.make_async_copy(w_in_ref.at[:, pl.ds(pl.multiple_of(core * HALF, HALF), HALF)], w1.at[0], load_sem.at[1]),
        pltpu.make_async_copy(w_out_ref.at[pl.ds(pl.multiple_of((1 - core) * HALF, HALF), HALF)], s2, load_sem.at[2]),
        pltpu.make_async_copy(w_out_ref.at[pl.ds(pl.multiple_of(core * HALF, HALF), HALF)], w2.at[0], load_sem.at[3]),
        pltpu.make_async_copy(cot_ref, xg.at[0, 0, 1], load_sem.at[4]),
    ]
    for load in loads:
        load.start()

    barrier = pltpu.get_barrier_semaphore()
    for device in [*col_mate, hop_mate, *z_mate]:
        pl.semaphore_signal(barrier, inc=1, device_id=device, device_id_type=MESH)

    for c in range(16):
        block = inputs_ref[:, c * FEAT : (c + 1) * FEAT].astype(F32)
        a2a_send[c] = jnp.concatenate([block[:, : FEAT // 2], block[:, FEAT // 2 :]], axis=0).astype(BF16)
    pl.semaphore_wait(barrier, 19)

    def a2a_copy(d):
        to = (col + d) % 16
        return remote(a2a_send.at[to], a2a_recv.at[col], a_ssem.at[d - 1], a_rsem.at[d - 1], (row, to))

    for d in range(1, 16):
        a2a_copy(d).start()
    a2a_recv[col] = a2a_send[col]

    mask_in = mask_in_ref[...].astype(F32).astype(BF16)
    m_in[0] = jnp.dot(mask_in, one_hot((48, HALF), 1, 6, core * 24), preferred_element_type=F32)
    m_in[1] = jnp.dot(mask_in, one_hot((48, HALF), 1, 6, (1 - core) * 24), preferred_element_type=F32)
    mask_out = mask_out_ref[...].astype(F32).astype(BF16)
    m_out[...] = jnp.dot(mask_out, one_hot((12, FEAT), 1, 6, 0), preferred_element_type=F32)

    def mask_rows(weight, rows, masks, first):
        def step(i, carry):
            here = pl.ds(pl.multiple_of(i * 64, 64), 64)
            keep = jnp.broadcast_to(masks[pl.ds(first + i, 1), :], (64, masks.shape[1])).astype(BF16)
            weight[here, :] = weight[here, :] * keep
            return carry

        lax.fori_loop(0, rows, step, 0)

    loads[0].wait()
    mask_rows(s1, 12, m_in.at[1], 0)
    give_in = remote(s1, w1.at[1], wsend_sem.at[0], wrecv_sem.at[0], sibling)
    give_in.start()
    loads[1].wait()
    mask_rows(w1.at[0], 12, m_in.at[0], 0)
    loads[2].wait()
    mask_rows(s2, 24, m_out, (1 - core) * 24)
    give_out = remote(s2, w2.at[1], wsend_sem.at[1], wrecv_sem.at[1], sibling)
    give_out.start()
    loads[3].wait()
    mask_rows(w2.at[0], 24, m_out, core * 24)
    loads[4].wait()

    for d in range(1, 16):
        a2a_copy(d).wait_recv()
    for pair in range(8):
        rows = []
        for c in (2 * pair, 2 * pair + 1):
            block = a2a_recv[c].astype(F32)
            rows.append(jnp.concatenate([block[:8], block[8:]], axis=1))
        xg[0, 0, 0, pair * 16 : (pair + 1) * 16, :] = jnp.concatenate(rows, axis=0).astype(BF16)

    def forward(s):
        return remote(xg.at[0, s], xg.at[1, s], f_ssem.at[s], f_rsem.at[s], sibling)

    def group_copy(source, target, device):
        return remote(xg.at[0, source], xg.at[0, target], g_ssem.at[target], g_rsem.at[target], device)

    forward(0).start()
    group_copy(0, 1, hop_mate).start()
    for d in (1, 2, 3):
        group_copy(0, 4 + d, z_mate[d - 1]).start()

    give_in.wait_recv()
    give_out.wait_recv()

    def rs1_copies(s):
        two = s % 2
        far = pl.ds(pl.multiple_of((1 - x) * 64, 64), 64)
        copies = [
            remote(rs1_send.at[two, :, far, 0:XW], r1x.at[s], rs1_ss.at[two, 0], rs1_rs.at[s, 0], x_mate)
        ]
        for d in (1, 2, 3):
            there = pl.ds(pl.multiple_of(flip(y, d) * 32, 32), 32)
            copies.append(
                remote(rs1_send.at[two, :, there, XW:HALF], r1y.at[s, d - 1], rs1_ss.at[two, d], rs1_rs.at[s, d], y_mate[d - 1])
            )
        return copies

    def rs2_copies(s):
        two = s % 2
        far = pl.ds(pl.multiple_of((1 - x) * 16, 16), 16)
        copies = [remote(rs2_sy.at[two, :, far], r2x.at[s], rs2_ss.at[two, 0], rs2_rs.at[s, 0], x_mate)]
        for d in (1, 2, 3):
            there = pl.ds(pl.multiple_of(flip(y, d) * 16, 16), 16)
            copies.append(
                remote(rs2_sx.at[two, :, there], r2y.at[s, d - 1], rs2_ss.at[two, d], rs2_rs.at[s, d], y_mate[d - 1])
            )
        return copies

    def ag1_copies(s):
        two = s % 2
        by_x = ahg.at[s, :, pl.ds(pl.multiple_of(x * 64 + y * 16, 16), 16), 0:XW]
        by_y = ahg.at[s, :, pl.ds(pl.multiple_of(y * 32 + x * 16, 16), 16), XW:HALF]
        copies = [remote(by_y, by_y, ag1_ss.at[two, 0], ag1_rs.at[s, 0], x_mate)]
        for d in (1, 2, 3):
            copies.append(remote(by_x, by_x, ag1_ss.at[two, d], ag1_rs.at[s, d], y_mate[d - 1]))
        return copies

    def ag2_copies(s):
        two = s % 2
        by_x = ahg.at[s, :, pl.ds(pl.multiple_of(x * 64, 64), 64), 0:XW]
        by_y = ahg.at[s, :, pl.ds(pl.multiple_of(y * 32, 32), 32), XW:HALF]
        copies = [remote(by_x, by_x, ag2_ss.at[two, 0], ag2_rs.at[s, 0], x_mate)]
        for d in (1, 2, 3):
            copies.append(remote(by_y, by_y, ag2_ss.at[two, d], ag2_rs.at[s, d], y_mate[d - 1]))
        return copies

    def sib_copy(s):
        two = s % 2
        return remote(sib_send.at[two], sib_recv.at[s], sib_ss.at[two], sib_rs.at[s], sibling)

    def keep_copy(s):
        return pltpu.make_async_copy(ahg.at[s], ahg_out.at[core, s], keep_sem.at[s])

    def give_copy(s):
        return remote(ahg.at[s], ahg_out.at[core, s], give_ss.at[s], give_rs.at[s], sibling)

    def row_copy(s):
        two = s % 2
        by = jnp.where(s < 5, s - 1, s - 4)
        return remote(row_send.at[two], row_recv.at[s], row_ss.at[two], row_rs.at[s], (flip(z, by) * 2 + xh, col))

    def multiply(s):
        two = s % 2
        forward(s).wait_recv()
        for j in range(HALF // TILE):
            here = slice(j * TILE, (j + 1) * TILE)
            total = jnp.dot(xg[0, s, 0], w1[0, :, here], preferred_element_type=F32)
            total += jnp.dot(xg[1, s, 0], w1[1, :, here], preferred_element_type=F32)
            part[two, 0, :, here] = total
            rs1_send[two, 0, :, here] = total.astype(BF16)
        for j in range(HALF // TILE):
            here = slice(j * TILE, (j + 1) * TILE)
            dims = (((1,), (1,)), ((), ()))
            total = lax.dot_general(xg[0, s, 1], w2[0, here, :], dims, preferred_element_type=F32)
            total += lax.dot_general(xg[1, s, 1], w2[1, here, :], dims, preferred_element_type=F32)
            part[two, 1, :, here] = total
            rs1_send[two, 1, :, here] = total.astype(BF16)
        for copy in rs1_copies(s):
            copy.start()

    def receive(s):
        group_copy(0, s, hop_mate).wait_recv()
        forward(s).start()

        @pl.when(s == 1)
        def _():
            for d in (1, 2, 3):
                group_copy(1, 1 + d, z_mate[d - 1]).start()

    def add_first(s):
        two = s % 2
        for copy in rs1_copies(s):
            copy.wait_recv()
        for k in (0, 1):
            total = part[two, k, pl.ds(pl.multiple_of(x * 64, 64), 64), 0:XW] + r1x[s, k].astype(F32)
            sum_x[two, k] = total
            rs2_sx[two, k] = total.astype(BF16)
            total = part[two, k, pl.ds(pl.multiple_of(y * 32, 32), 32), XW:HALF]
            for d in range(3):
                total += r1y[s, d, k].astype(F32)
            sum_y[two, k] = total
            rs2_sy[two, k] = total.astype(BF16)
        for copy in rs2_copies(s):
            copy.start()

    def activate(s):
        two = s % 2
        for copy in rs1_copies(s):
            copy.wait_send()
        for copy in rs2_copies(s):
            copy.wait_recv()
        by_x, by_y = [], []
        for k in (0, 1):
            total = sum_x[two, k, pl.ds(pl.multiple_of(y * 16, 16), 16), :]
            for d in range(3):
                total += r2y[s, d, k].astype(F32)
            by_x.append(total)
            by_y.append(sum_y[two, k, pl.ds(pl.multiple_of(x * 16, 16), 16), :] + r2x[s, k].astype(F32))
        for k, values in enumerate(gelu_parts(*by_x)):
            ahg[s, k, pl.ds(pl.multiple_of(x * 64 + y * 16, 16), 16), 0:XW] = values.astype(BF16)
        for k, values in enumerate(gelu_parts(*by_y)):
            ahg[s, k, pl.ds(pl.multiple_of(y * 32 + x * 16, 16), 16), XW:HALF] = values.astype(BF16)
        for copy in ag1_copies(s):
            copy.start()

    def spread(s):
        for copy in rs2_copies(s):
            copy.wait_send()
        for copy in ag1_copies(s):
            copy.wait_recv()
        for copy in ag2_copies(s):
            copy.start()
        for copy in ag1_copies(s):
            copy.wait_send()

    def project(s):
        two = s % 2
        for copy in ag2_copies(s):
            copy.wait()
        keep_copy(s).start()
        give_copy(s).start()
        for j in range(FEAT // TILE):
            here = slice(j * TILE, (j + 1) * TILE)
            dims = (((1,), (1,)), ((), ()))
            sib_send[two, 0, :, here] = jnp.dot(ahg[s, 0], w2[1, :, here], preferred_element_type=F32).astype(BF16)
            sib_send[two, 1, :, here] = lax.dot_general(
                ahg[s, 1], w1[1, here, :], dims, preferred_element_type=F32
            ).astype(BF16)
        sib_copy(s).start()
        for j in range(FEAT // TILE):
            here = slice(j * TILE, (j + 1) * TILE)
            dims = (((1,), (1,)), ((), ()))
            prod[two, 0, :, here] = jnp.dot(ahg[s, 0], w2[0, :, here], preferred_element_type=F32)
            prod[two, 1, :, here] = lax.dot_general(ahg[s, 1], w1[0, here, :], dims, preferred_element_type=F32)

    def hand_on(s):
        two = s % 2
        sib_copy(s).wait_send()
        sib_copy(s).wait_recv()

        @pl.when(s < 2)
        def _():
            row_own[s] = prod[two] + sib_recv[s].astype(F32)

        @pl.when(s >= 2)
        def _():
            row_send[two] = (prod[two] + sib_recv[s].astype(F32)).astype(BF16)
            row_copy(s).start()

    def finish(s):
        keep_copy(s).wait()
        give_copy(s).wait()

        @pl.when(s >= 2)
        def _():
            row_copy(s).wait_send()

    hop_copy = remote(hop_send, hop_recv, hop_ss, hop_rs, hop_mate)

    def step(t, carry):
        def at(lag, stage):
            pl.when(jnp.logical_and(t >= lag, t < GROUPS + lag))(lambda: stage(t - lag))

        at(6, finish)
        at(3, spread)
        at(2, activate)
        at(1, add_first)
        at(0, multiply)
        pl.when(t < GROUPS - 1)(lambda: receive(t + 1))
        at(4, project)
        at(5, hand_on)

        @pl.when(t == 11)
        def _():
            total = row_own[1]
            for s in (2, 3, 4):
                row_copy(s).wait_recv()
                total += row_recv[s].astype(F32)
            hop_send[...] = total.astype(BF16)
            hop_copy.start()

        return carry

    lax.fori_loop(0, GROUPS + 6, step, 0)

    total = row_own[0]
    for s in (5, 6, 7):
        row_copy(s).wait_recv()
        total += row_recv[s].astype(F32)
    hop_copy.wait()
    total += hop_recv[...].astype(F32)
    out_ref[...] = total[0].astype(BF16)
    ig_ref[...] = total[1].astype(BF16)

    keep_x = pltpu.make_async_copy(xg.at[0], xg_out, load_sem.at[0])
    keep_x.start()
    give_in.wait_send()
    give_out.wait_send()
    for d in range(1, 16):
        a2a_copy(d).wait_send()
    for s in range(GROUPS):
        forward(s).wait_send()
    for s in range(1, GROUPS):
        group_copy(0, s, hop_mate).wait_send()
    keep_x.wait()


def run_pipeline(inputs, cotangent, w_in, w_out, mask_in, mask_out):
    vmem = pl.BlockSpec(memory_space=pltpu.VMEM)
    hbm = pl.BlockSpec(memory_space=pltpu.HBM)
    dma = pltpu.SemaphoreType.DMA
    return pl.pallas_call(
        pipeline,
        out_shape=[
            jax.ShapeDtypeStruct((GROUP, FEAT), BF16),
            jax.ShapeDtypeStruct((GROUP, FEAT), BF16),
            jax.ShapeDtypeStruct((GROUPS, 2, GROUP, FEAT), BF16),
            jax.ShapeDtypeStruct((2, GROUPS, 2, GROUP, HALF), BF16),
        ],
        in_specs=[vmem, hbm, hbm, hbm, vmem, vmem],
        out_specs=[vmem, vmem, hbm, hbm],
        scratch_shapes=[
            pltpu.VMEM((2, FEAT, HALF), BF16),
            pltpu.VMEM((2, HALF, FEAT), BF16),
            pltpu.VMEM((FEAT, HALF), BF16),
            pltpu.VMEM((HALF, FEAT), BF16),
            pltpu.VMEM((2, 12, HALF), F32),
            pltpu.VMEM((48, FEAT), F32),
            pltpu.VMEM((16, 16, FEAT // 2), BF16),
            pltpu.VMEM((16, 16, FEAT // 2), BF16),
            pltpu.VMEM((2, GROUPS, 2, GROUP, FEAT), BF16),
            pltpu.VMEM((2, 2, GROUP, HALF), F32),
            pltpu.VMEM((2, 2, GROUP, HALF), BF16),
            pltpu.VMEM((GROUPS, 2, 64, XW), BF16),
            pltpu.VMEM((GROUPS, 3, 2, 32, YW), BF16),
            pltpu.VMEM((2, 2, 64, XW), F32),
            pltpu.VMEM((2, 2, 32, YW), F32),
            pltpu.VMEM((2, 2, 64, XW), BF16),
            pltpu.VMEM((2, 2, 32, YW), BF16),
            pltpu.VMEM((GROUPS, 3, 2, 16, XW), BF16),
            pltpu.VMEM((GROUPS, 2, 16, YW), BF16),
            pltpu.VMEM((GROUPS, 2, GROUP, HALF), BF16),
            pltpu.VMEM((2, 2, GROUP, FEAT), F32),
            pltpu.VMEM((2, 2, GROUP, FEAT), BF16),
            pltpu.VMEM((GROUPS, 2, GROUP, FEAT), BF16),
            pltpu.VMEM((2, 2, GROUP, FEAT), BF16),
            pltpu.VMEM((GROUPS, 2, GROUP, FEAT), BF16),
            pltpu.VMEM((2, 2, GROUP, FEAT), F32),
            pltpu.VMEM((2, GROUP, FEAT), BF16),
            pltpu.VMEM((2, GROUP, FEAT), BF16),
            dma((5,)), dma((2,)), dma((2,)),
            dma((15,)), dma((15,)),
            dma((GROUPS,)), dma((GROUPS,)), dma((GROUPS,)), dma((GROUPS,)),
            dma((2, 4)), dma((GROUPS, 4)), dma((2, 4)), dma((GROUPS, 4)),
            dma((2, 4)), dma((GROUPS, 4)), dma((2, 4)), dma((GROUPS, 4)),
            dma((2,)), dma((GROUPS,)), dma((2,)), dma((GROUPS,)),
            dma((GROUPS,)), dma((GROUPS,)), dma((GROUPS,)),
            dma, dma,
        ],
        compiler_params=pltpu.CompilerParams(
            collective_id=1, has_side_effects=True, vmem_limit_bytes=60 << 20
        ),
        cost_estimate=pl.CostEstimate(flops=20 << 30, bytes_accessed=30 << 20, transcendentals=1 << 20),
    )(inputs, cotangent, w_in, w_out, mask_in, mask_out)


WIDTH = 512


def weight_grads(x_ref, g_ref, a_ref, h_ref, mask_in_ref, mask_out_ref, w_in_ref, w_out_ref):
    j = pl.program_id(0)
    dims = (((0,), (0,)), ((), ()))
    tokens = GROUP * GROUPS

    mask = mask_in_ref[...].astype(F32).astype(BF16)
    keep = jnp.dot(one_hot((FEAT, 12), 0, 6, 0), mask, preferred_element_type=F32).astype(BF16)
    keep = jnp.dot(keep, one_hot((48, WIDTH), 1, 6, j * (WIDTH // 64)), preferred_element_type=F32)
    product = lax.dot_general(
        x_ref[...].reshape(tokens, FEAT), h_ref[...].reshape(tokens, WIDTH), dims, preferred_element_type=F32
    )
    w_in_ref[...] = (product * keep).astype(BF16)

    mask = mask_out_ref[...].astype(F32).astype(BF16)
    keep = jnp.dot(one_hot((WIDTH, 48), 0, 6, j * (WIDTH // 64)), mask, preferred_element_type=F32).astype(BF16)
    keep = jnp.dot(keep, one_hot((12, FEAT), 1, 6, 0), preferred_element_type=F32)
    product = lax.dot_general(
        a_ref[...].reshape(tokens, WIDTH), g_ref[...].reshape(tokens, FEAT), dims, preferred_element_type=F32
    )
    w_out_ref[...] = (product * keep).astype(BF16)


def run_weight_grads(xg, ahg, mask_in, mask_out):
    per = HALF // WIDTH

    def values(k):
        return pl.BlockSpec((GROUPS, None, GROUP, FEAT), lambda j: (0, k, 0, 0))

    def hidden(k):
        return pl.BlockSpec((None, GROUPS, None, GROUP, WIDTH), lambda j: (j // per, 0, k, 0, j % per))

    return pl.pallas_call(
        weight_grads,
        grid=(2 * per,),
        out_shape=[
            jax.ShapeDtypeStruct((FEAT, 2 * HALF), BF16),
            jax.ShapeDtypeStruct((2 * HALF, FEAT), BF16),
        ],
        in_specs=[
            values(0), values(1), hidden(0), hidden(1),
            pl.BlockSpec((12, 48), lambda j: (0, 0)), pl.BlockSpec((48, 12), lambda j: (0, 0)),
        ],
        out_specs=[pl.BlockSpec((FEAT, WIDTH), lambda j: (0, j)), pl.BlockSpec((WIDTH, FEAT), lambda j: (j, 0))],
        compiler_params=pltpu.CompilerParams(vmem_limit_bytes=48 << 20),
        cost_estimate=pl.CostEstimate(flops=10 << 30, bytes_accessed=25 << 20, transcendentals=0),
    )(xg, xg, ahg, ahg, mask_in, mask_out)


def body(inputs, cotangent, w_in, w_out, mask_in, mask_out):
    output, input_grad, xg, ahg = run_pipeline(inputs, cotangent, w_in, w_out, mask_in, mask_out)
    w_in_grad, w_out_grad = run_weight_grads(xg, ahg, mask_in, mask_out)
    return (output, input_grad, w_in_grad, w_out_grad)


def solution(mesh):
    in_specs = (
        P(("row", "col"), None),
        P("row", "col"),
        P("col", "row"),
        P("row", "col"),
        P("col", "row"),
        P("row", "col"),
    )
    out_specs = (P("row", "col"), P("row", "col"), P("col", "row"), P("row", "col"))
    return jax.shard_map(body, mesh=mesh, in_specs=in_specs, out_specs=out_specs, check_vma=False)
```

```python
import functools

import jax
import jax.numpy as jnp
from jax import lax
from jax.experimental import pallas as pl
from jax.experimental.pallas import tpu as pltpu
from jax.sharding import PartitionSpec as P

MESH = pl.DeviceIdType.MESH
F32 = jnp.float32
BF16 = jnp.bfloat16

GROUP = 128
GROUPS = 8
UNITS = 2 * GROUPS
FEAT = 768
COLS = 768
XW = 384
YW = COLS - XW
TILE = 256
NT = (((1,), (1,)), ((), ()))
TN = (((0,), (0,)), ((), ()))


def flip(position, by):
    return (position % 2 + by % 2) % 2 + 2 * ((position // 2 + by // 2) % 2)


def one_hot(shape, along, shift, offset):
    wide = lax.broadcasted_iota(jnp.int32, shape, along)
    other = lax.broadcasted_iota(jnp.int32, shape, 1 - along)
    return (lax.shift_right_logical(wide, shift) + offset == other).astype(F32).astype(BF16)


def gelu_parts(hidden, act_grad):
    c = 0.7978845608028654
    square = hidden * hidden
    inner = jnp.tanh(c * hidden * (1.0 + 0.044715 * square))
    cdf = 0.5 * (1.0 + inner)
    slope = cdf + 0.5 * hidden * (1.0 - inner * inner) * (c * (1.0 + 0.134145 * square))
    return hidden * cdf, act_grad * slope


def pipeline(
    inputs_ref, cot_ref, w_in_ref, w_out_ref, mask_in_ref, mask_out_ref,
    out_ref, ig_ref, xt_out, g_out, at_out, hg_out,
    w1, w2, s1, s2, m_in, m_out, a2a_send, a2a_recv, xg, part, rs1_send,
    r1x, r1y, sum_x, sum_y, rs2_sx, rs2_sy, r2y, r2x, ahg, prod, sib_send, sib_recv,
    row_send, row_recv, row_own, hop_send, hop_recv, at_buf, xt_buf,
    load_sem, wsend_sem, wrecv_sem, a_ssem, a_rsem, g_ssem, g_rsem, f_ssem, f_rsem,
    rs1_ss, rs1_rs, rs2_ss, rs2_rs, ag1_ss, ag1_rs, ag2_ss, ag2_rs,
    sib_ss, sib_rs, row_ss, row_rs, keep_sem, give_ss, give_rs, store_sem, hop_ss, hop_rs,
):
    row, col = lax.axis_index("row"), lax.axis_index("col")
    z, xh = row // 2, row % 2
    chip, core = col // 2, col % 2
    y, x = chip // 2, chip % 2

    sibling = (row, chip * 2 + 1 - core)
    x_mate = (row, (y * 2 + 1 - x) * 2 + core)
    y_mate = [(row, (flip(y, d) * 2 + x) * 2 + core) for d in (1, 2, 3)]
    hop_mate = (z * 2 + 1 - xh, col)
    z_mate = [(flip(z, d) * 2 + xh, col) for d in (1, 2, 3)]
    col_mate = [(row, (col + d) % 16) for d in range(1, 16)]

    def remote(source, target, send, recv, device):
        return pltpu.make_async_remote_copy(
            src_ref=source, dst_ref=target, send_sem=send, recv_sem=recv,
            device_id=device, device_id_type=MESH,
        )

    def part_of(base, u):
        return pl.ds(pl.multiple_of(base * 2 * COLS + u * COLS, COLS), COLS)

    loads = []
    for u in (0, 1):
        loads += [
            (w_out_ref.at[part_of(1 - core, u), :], s2.at[u]),
            (w_in_ref.at[:, part_of(1 - core, u)], s1.at[u]),
            (w_out_ref.at[part_of(core, u), :], w2.at[0, u]),
            (w_in_ref.at[:, part_of(core, u)], w1.at[0, u]),
        ]
    loads.append((cot_ref, xg.at[0, GROUPS - 1, 1]))
    loads = [pltpu.make_async_copy(*pair, load_sem.at[i]) for i, pair in enumerate(loads)]
    for load in loads:
        load.start()

    barrier = pltpu.get_barrier_semaphore()
    for device in [*col_mate, hop_mate, *z_mate]:
        pl.semaphore_signal(barrier, inc=1, device_id=device, device_id_type=MESH)

    for c in range(16):
        block = inputs_ref[:, c * FEAT : (c + 1) * FEAT].astype(F32)
        a2a_send[c] = jnp.concatenate([block[:, : FEAT // 2], block[:, FEAT // 2 :]], axis=0).astype(BF16)
    pl.semaphore_wait(barrier, 19)

    def a2a_copy(d):
        to = (col + d) % 16
        return remote(a2a_send.at[to], a2a_recv.at[col], a_ssem.at[d - 1], a_rsem.at[d - 1], (row, to))

    for d in range(1, 16):
        a2a_copy(d).start()
    a2a_recv[col] = a2a_send[col]

    def group_copy(source, target, k, device):
        return remote(xg.at[0, source, k], xg.at[0, target, k], g_ssem.at[target, k], g_rsem.at[target, k], device)

    def forward(s):
        return remote(xg.at[0, s], xg.at[1, s], f_ssem.at[s], f_rsem.at[s], sibling)

    mask_in = mask_in_ref[...].astype(F32).astype(BF16)
    m_in[0] = jnp.dot(mask_in, one_hot((48, 2 * COLS), 1, 6, core * 24), preferred_element_type=F32)
    m_in[1] = jnp.dot(mask_in, one_hot((48, 2 * COLS), 1, 6, (1 - core) * 24), preferred_element_type=F32)
    mask_out = mask_out_ref[...].astype(F32).astype(BF16)
    m_out[...] = lax.dot_general(mask_out, one_hot((12, FEAT), 1, 6, 0), TN, preferred_element_type=F32)

    def mask_rows(weight, masks, first, columns):
        def step(i, carry):
            here = pl.ds(pl.multiple_of(i * 64, 64), 64)
            keep = jnp.broadcast_to(masks[pl.ds(first + i, 1), columns], (64, COLS)).astype(BF16)
            weight[here, :] = weight[here, :] * keep
            return carry

        lax.fori_loop(0, 12, step, 0)

    gives = []
    loads[8].wait()
    group_copy(7, 0, 1, z_mate[0]).start()
    group_copy(7, 1, 1, hop_mate).start()
    for u in (0, 1):
        columns = slice(u * COLS, (u + 1) * COLS)
        loads[4 * u].wait()
        mask_rows(s2.at[u], m_out, (1 - core) * 24 + u * 12, slice(None))
        gives.append(remote(s2.at[u], w2.at[1, u], wsend_sem.at[2 * u], wrecv_sem.at[2 * u], sibling))
        gives[-1].start()
        loads[4 * u + 1].wait()
        mask_rows(s1.at[u], m_in.at[1], 0, columns)
        gives.append(remote(s1.at[u], w1.at[1, u], wsend_sem.at[2 * u + 1], wrecv_sem.at[2 * u + 1], sibling))
        gives[-1].start()

    for d in range(1, 16):
        a2a_copy(d).wait_recv()
    for pair in range(8):
        rows = []
        for c in (2 * pair, 2 * pair + 1):
            block = a2a_recv[c].astype(F32)
            rows.append(jnp.concatenate([block[:8], block[8:]], axis=1))
        xg[0, 7, 0, pair * 16 : (pair + 1) * 16, :] = jnp.concatenate(rows, axis=0).astype(BF16)
    group_copy(7, 0, 0, z_mate[0]).start()
    group_copy(7, 1, 0, hop_mate).start()

    for u in (0, 1):
        loads[4 * u + 2].wait()
        mask_rows(w2.at[0, u], m_out, core * 24 + u * 12, slice(None))
        loads[4 * u + 3].wait()
        mask_rows(w1.at[0, u], m_in.at[0], 0, slice(u * COLS, (u + 1) * COLS))

    for k in (0, 1):
        group_copy(7, 0, k, z_mate[0]).wait_recv()
    forward(0).start()
    for give in gives:
        give.wait_recv()

    def rs1_copies(n):
        two = n % 2
        far = pl.ds(pl.multiple_of((1 - x) * 64, 64), 64)
        copies = [remote(rs1_send.at[two, :, far, 0:XW], r1x.at[n], rs1_ss.at[two, 0], rs1_rs.at[n, 0], x_mate)]
        for d in (1, 2, 3):
            there = pl.ds(pl.multiple_of(flip(y, d) * 32, 32), 32)
            copies.append(
                remote(rs1_send.at[two, :, there, XW:COLS], r1y.at[n, d - 1], rs1_ss.at[two, d], rs1_rs.at[n, d], y_mate[d - 1])
            )
        return copies

    def rs2_copies(n):
        two = n % 2
        far = pl.ds(pl.multiple_of((1 - x) * 16, 16), 16)
        copies = [remote(rs2_sy.at[two, :, far], r2x.at[n], rs2_ss.at[two, 0], rs2_rs.at[n, 0], x_mate)]
        for d in (1, 2, 3):
            there = pl.ds(pl.multiple_of(flip(y, d) * 16, 16), 16)
            copies.append(
                remote(rs2_sx.at[two, :, there], r2y.at[n, d - 1], rs2_ss.at[two, d], rs2_rs.at[n, d], y_mate[d - 1])
            )
        return copies

    def ag1_copies(n):
        two = n % 2
        by_x = ahg.at[n, :, pl.ds(pl.multiple_of(x * 64 + y * 16, 16), 16), 0:XW]
        by_y = ahg.at[n, :, pl.ds(pl.multiple_of(y * 32 + x * 16, 16), 16), XW:COLS]
        copies = [remote(by_y, by_y, ag1_ss.at[two, 0], ag1_rs.at[n, 0], x_mate)]
        for d in (1, 2, 3):
            copies.append(remote(by_x, by_x, ag1_ss.at[two, d], ag1_rs.at[n, d], y_mate[d - 1]))
        return copies

    def ag2_copies(n):
        two = n % 2
        by_x = ahg.at[n, :, pl.ds(pl.multiple_of(x * 64, 64), 64), 0:XW]
        by_y = ahg.at[n, :, pl.ds(pl.multiple_of(y * 32, 32), 32), XW:COLS]
        copies = [remote(by_x, by_x, ag2_ss.at[two, 0], ag2_rs.at[n, 0], x_mate)]
        for d in (1, 2, 3):
            copies.append(remote(by_y, by_y, ag2_ss.at[two, d], ag2_rs.at[n, d], y_mate[d - 1]))
        return copies

    def sib_copy(s):
        two = s % 2
        return remote(sib_send.at[two], sib_recv.at[s], sib_ss.at[two], sib_rs.at[s], sibling)

    def tokens_of(s):
        return pl.ds(pl.multiple_of(s * GROUP, GROUP), GROUP)

    def keep_copies(n):
        s, u, two = n // 2, n % 2, n % 2
        pairs = [(at_buf.at[two], at_out.at[core, u, :, tokens_of(s)]), (ahg.at[n, 1], hg_out.at[core, u, tokens_of(s), :])]
        copies = []
        for k, (source, target) in enumerate(pairs):
            copies.append(pltpu.make_async_copy(source, target, keep_sem.at[two, k]))
            copies.append(remote(source, target, give_ss.at[two, k], give_rs.at[n, k], sibling))
        return copies

    def store_copies(s):
        return [
            pltpu.make_async_copy(xt_buf, xt_out.at[:, tokens_of(s)], store_sem.at[0]),
            pltpu.make_async_copy(xg.at[0, s, 1], g_out.at[tokens_of(s), :], store_sem.at[1]),
        ]

    def row_copy(s):
        two = s % 2
        by = jnp.where(s == 0, 1, jnp.where(s < 5, s - 1, s - 3))
        return remote(row_send.at[two], row_recv.at[s], row_ss.at[two], row_rs.at[s], (flip(z, by) * 2 + xh, col))

    def multiply(n):
        s, u, two = n // 2, n % 2, n % 2

        @pl.when(u == 0)
        def _():
            forward(s).wait_recv()

        for j in range(COLS // TILE):
            here = slice(j * TILE, (j + 1) * TILE)
            total = lax.dot_general(xg[0, s, 1], w2[0, u, here, :], NT, preferred_element_type=F32)
            total += lax.dot_general(xg[1, s, 1], w2[1, u, here, :], NT, preferred_element_type=F32)
            part[two, 1, :, here] = total
            rs1_send[two, 1, :, here] = total.astype(BF16)
        for j in range(COLS // TILE):
            here = slice(j * TILE, (j + 1) * TILE)
            total = jnp.dot(xg[0, s, 0], w1[0, u, :, here], preferred_element_type=F32)
            total += jnp.dot(xg[1, s, 0], w1[1, u, :, here], preferred_element_type=F32)
            part[two, 0, :, here] = total
            rs1_send[two, 0, :, here] = total.astype(BF16)
        for copy in rs1_copies(n):
            copy.start()

    def receive(s):
        @pl.when(s < GROUPS - 1)
        def _():
            for k in (0, 1):
                group_copy(7, s, k, hop_mate).wait_recv()

        forward(s).start()
        for at, source, target, d in ((1, 1, 2, 1), (2, 1, 3, 2), (2, 1, 4, 3), (3, 7, 5, 2), (3, 7, 6, 3)):

            @pl.when(s == at)
            def _(source=source, target=target, d=d):
                for k in (0, 1):
                    group_copy(source, target, k, z_mate[d - 1]).start()

    def add_first(n):
        two = n % 2
        for copy in rs1_copies(n):
            copy.wait()
        for k in (0, 1):
            total = part[two, k, pl.ds(pl.multiple_of(x * 64, 64), 64), 0:XW] + r1x[n, k].astype(F32)
            sum_x[two, k] = total
            rs2_sx[two, k] = total.astype(BF16)
            total = part[two, k, pl.ds(pl.multiple_of(y * 32, 32), 32), XW:COLS]
            for d in range(3):
                total += r1y[n, d, k].astype(F32)
            sum_y[two, k] = total
            rs2_sy[two, k] = total.astype(BF16)
        for copy in rs2_copies(n):
            copy.start()

    def activate(n):
        two = n % 2
        for copy in rs2_copies(n):
            copy.wait()
        by_x, by_y = [], []
        for k in (0, 1):
            total = sum_x[two, k, pl.ds(pl.multiple_of(y * 16, 16), 16), :]
            for d in range(3):
                total += r2y[n, d, k].astype(F32)
            by_x.append(total)
            by_y.append(sum_y[two, k, pl.ds(pl.multiple_of(x * 16, 16), 16), :] + r2x[n, k].astype(F32))
        for k, values in enumerate(gelu_parts(*by_x)):
            ahg[n, k, pl.ds(pl.multiple_of(x * 64 + y * 16, 16), 16), 0:XW] = values.astype(BF16)
        for k, values in enumerate(gelu_parts(*by_y)):
            ahg[n, k, pl.ds(pl.multiple_of(y * 32 + x * 16, 16), 16), XW:COLS] = values.astype(BF16)
        for copy in ag1_copies(n):
            copy.start()

    def spread(n):
        for copy in ag1_copies(n):
            copy.wait()
        for copy in ag2_copies(n):
            copy.start()

    def project(n):
        s, u, two = n // 2, n % 2, (n // 2) % 2
        for copy in ag2_copies(n):
            copy.wait()

        def products(fc, here):
            return (
                jnp.dot(ahg[n, 0], w2[fc, u, :, here], preferred_element_type=F32),
                lax.dot_general(ahg[n, 1], w1[fc, u, here, :], NT, preferred_element_type=F32),
            )

        @pl.when(u == 0)
        def _():
            for fc in (1, 0):
                for j in range(FEAT // TILE):
                    here = slice(j * TILE, (j + 1) * TILE)
                    for k, value in enumerate(products(fc, here)):
                        prod[two, fc, k, :, here] = value

        @pl.when(u == 1)
        def _():
            for j in range(FEAT // TILE):
                here = slice(j * TILE, (j + 1) * TILE)
                for k, value in enumerate(products(1, here)):
                    sib_send[two, k, :, here] = (prod[two, 1, k, :, here] + value).astype(BF16)
            sib_copy(s).start()
            for j in range(FEAT // TILE):
                here = slice(j * TILE, (j + 1) * TILE)
                for k, value in enumerate(products(0, here)):
                    prod[two, 0, k, :, here] += value

        at_buf[n % 2] = ahg[n, 0].T
        for copy in keep_copies(n):
            copy.start()

        @pl.when(u == 0)
        def _():
            xt_buf[...] = xg[0, s, 0].T
            for copy in store_copies(s):
                copy.start()

    def hand_on(n):
        s, two = n // 2, (n // 2) % 2

        @pl.when(n % 2 == 1)
        def _():
            sib_copy(s).wait()

            @pl.when(jnp.logical_or(s == 1, s == 7))
            def _():
                row_own[jnp.where(s == 1, 1, 0)] = prod[two, 0] + sib_recv[s].astype(F32)

            @pl.when(jnp.logical_and(s != 1, s != 7))
            def _():
                row_send[two] = (prod[two, 0] + sib_recv[s].astype(F32)).astype(BF16)
                row_copy(s).start()

    def finish(n):
        s = n // 2
        for copy in keep_copies(n):
            copy.wait()

        @pl.when(n % 2 == 0)
        def _():
            for copy in store_copies(s):
                copy.wait()

    def settle(n):
        s = n // 2

        @pl.when(jnp.logical_and(n % 2 == 1, jnp.logical_and(s != 1, s != 7)))
        def _():
            row_copy(s).wait_send()

    hop_copy = remote(hop_send, hop_recv, hop_ss, hop_rs, hop_mate)

    def step(t, carry):
        def at(lag, stage):
            pl.when(jnp.logical_and(t >= lag, t < UNITS + lag))(lambda: stage(t - lag))

        at(0, multiply)
        at(1, add_first)
        at(2, activate)
        at(3, spread)

        @pl.when(jnp.logical_and(t % 2 == 0, t < UNITS - 2))
        def _():
            receive(t // 2 + 1)

        at(5, finish)
        at(4, project)
        at(7, settle)
        at(5, hand_on)

        @pl.when(t == 16)
        def _():
            total = row_own[1]
            for s in (2, 3, 4):
                row_copy(s).wait_recv()
                total += row_recv[s].astype(F32)
            hop_send[...] = total.astype(BF16)
            hop_copy.start()

        return carry

    lax.fori_loop(0, UNITS + 5, step, 0)

    total = row_own[0]
    for s in (0, 5, 6):
        row_copy(s).wait_recv()
        total += row_recv[s].astype(F32)
    hop_copy.wait()
    total += hop_recv[...].astype(F32)
    out_ref[...] = total[0].astype(BF16)
    ig_ref[...] = total[1].astype(BF16)

    for give in gives:
        give.wait_send()
    for d in range(1, 16):
        a2a_copy(d).wait_send()
    for s in range(GROUPS):
        forward(s).wait_send()
    for s in range(GROUPS - 1):
        for k in (0, 1):
            group_copy(7, s, k, hop_mate).wait_send()


def run_pipeline(inputs, cotangent, w_in, w_out, mask_in, mask_out):
    vmem = pl.BlockSpec(memory_space=pltpu.VMEM)
    hbm = pl.BlockSpec(memory_space=pltpu.HBM)
    dma = pltpu.SemaphoreType.DMA
    tokens = GROUP * GROUPS
    return pl.pallas_call(
        pipeline,
        out_shape=[
            jax.ShapeDtypeStruct((GROUP, FEAT), BF16),
            jax.ShapeDtypeStruct((GROUP, FEAT), BF16),
            jax.ShapeDtypeStruct((FEAT, tokens), BF16),
            jax.ShapeDtypeStruct((tokens, FEAT), BF16),
            jax.ShapeDtypeStruct((2, 2, COLS, tokens), BF16),
            jax.ShapeDtypeStruct((2, 2, tokens, COLS), BF16),
        ],
        in_specs=[vmem, hbm, hbm, hbm, vmem, vmem],
        out_specs=[vmem, vmem, hbm, hbm, hbm, hbm],
        scratch_shapes=[
            pltpu.VMEM((2, 2, FEAT, COLS), BF16),
            pltpu.VMEM((2, 2, COLS, FEAT), BF16),
            pltpu.VMEM((2, FEAT, COLS), BF16),
            pltpu.VMEM((2, COLS, FEAT), BF16),
            pltpu.VMEM((2, 12, 2 * COLS), F32),
            pltpu.VMEM((48, FEAT), F32),
            pltpu.VMEM((16, 16, FEAT // 2), BF16),
            pltpu.VMEM((16, 16, FEAT // 2), BF16),
            pltpu.VMEM((2, GROUPS, 2, GROUP, FEAT), BF16),
            pltpu.VMEM((2, 2, GROUP, COLS), F32),
            pltpu.VMEM((2, 2, GROUP, COLS), BF16),
            pltpu.VMEM((UNITS, 2, 64, XW), BF16),
            pltpu.VMEM((UNITS, 3, 2, 32, YW), BF16),
            pltpu.VMEM((2, 2, 64, XW), F32),
            pltpu.VMEM((2, 2, 32, YW), F32),
            pltpu.VMEM((2, 2, 64, XW), BF16),
            pltpu.VMEM((2, 2, 32, YW), BF16),
            pltpu.VMEM((UNITS, 3, 2, 16, XW), BF16),
            pltpu.VMEM((UNITS, 2, 16, YW), BF16),
            pltpu.VMEM((UNITS, 2, GROUP, COLS), BF16),
            pltpu.VMEM((2, 2, 2, GROUP, FEAT), F32),
            pltpu.VMEM((2, 2, GROUP, FEAT), BF16),
            pltpu.VMEM((GROUPS, 2, GROUP, FEAT), BF16),
            pltpu.VMEM((2, 2, GROUP, FEAT), BF16),
            pltpu.VMEM((GROUPS, 2, GROUP, FEAT), BF16),
            pltpu.VMEM((2, 2, GROUP, FEAT), F32),
            pltpu.VMEM((2, GROUP, FEAT), BF16),
            pltpu.VMEM((2, GROUP, FEAT), BF16),
            pltpu.VMEM((2, COLS, GROUP), BF16),
            pltpu.VMEM((FEAT, GROUP), BF16),
            dma((9,)), dma((4,)), dma((4,)),
            dma((15,)), dma((15,)),
            dma((GROUPS, 2)), dma((GROUPS, 2)), dma((GROUPS,)), dma((GROUPS,)),
            dma((2, 4)), dma((UNITS, 4)), dma((2, 4)), dma((UNITS, 4)),
            dma((2, 4)), dma((UNITS, 4)), dma((2, 4)), dma((UNITS, 4)),
            dma((2,)), dma((GROUPS,)), dma((2,)), dma((GROUPS,)),
            dma((2, 2)), dma((2, 2)), dma((UNITS, 2)), dma((2,)),
            dma, dma,
        ],
        compiler_params=pltpu.CompilerParams(
            collective_id=1, has_side_effects=True, vmem_limit_bytes=60 << 20
        ),
        cost_estimate=pl.CostEstimate(flops=20 << 30, bytes_accessed=30 << 20, transcendentals=1 << 20),
    )(inputs, cotangent, w_in, w_out, mask_in, mask_out)


def weight_grads(
    xt_ref, g_ref, at_ref, hg_ref, mask_in_ref, mask_out_ref, out_in, ig_in, w_in_ref, w_out_ref, out_ref, ig_ref
):
    j = pl.program_id(0)

    @pl.when(j == 0)
    def _():
        out_ref[...] = out_in[...]
        ig_ref[...] = ig_in[...]

    mask = mask_in_ref[...].astype(F32).astype(BF16)
    keep = jnp.dot(one_hot((FEAT, 12), 0, 6, 0), mask, preferred_element_type=F32).astype(BF16)
    keep = jnp.dot(keep, one_hot((48, COLS), 1, 6, j * (COLS // 64)), preferred_element_type=F32)
    w_in_ref[...] = (jnp.dot(xt_ref[...], hg_ref[...], preferred_element_type=F32) * keep).astype(BF16)

    mask = mask_out_ref[...].astype(F32).astype(BF16)
    keep = lax.dot_general(one_hot((COLS, 48), 0, 6, j * (COLS // 64)), mask, NT, preferred_element_type=F32).astype(BF16)
    keep = jnp.dot(keep, one_hot((12, FEAT), 1, 6, 0), preferred_element_type=F32)
    w_out_ref[...] = (jnp.dot(at_ref[...], g_ref[...], preferred_element_type=F32) * keep).astype(BF16)


def run_weight_grads(output, input_grad, xt, g, at, hg, mask_in, mask_out):
    tokens = GROUP * GROUPS

    def whole(*shape):
        return pl.BlockSpec(shape, lambda j: (0, 0))

    def tile(*shape):
        return pl.BlockSpec((None, None, *shape), lambda j: (j // 2, j % 2, 0, 0))

    return pl.pallas_call(
        weight_grads,
        grid=(4,),
        out_shape=[
            jax.ShapeDtypeStruct((FEAT, 4 * COLS), BF16),
            jax.ShapeDtypeStruct((4 * COLS, FEAT), BF16),
            jax.ShapeDtypeStruct((GROUP, FEAT), BF16),
            jax.ShapeDtypeStruct((GROUP, FEAT), BF16),
        ],
        in_specs=[
            whole(FEAT, tokens), whole(tokens, FEAT), tile(COLS, tokens), tile(tokens, COLS),
            whole(12, 48), whole(12, 48), whole(GROUP, FEAT), whole(GROUP, FEAT),
        ],
        out_specs=[
            pl.BlockSpec((FEAT, COLS), lambda j: (0, j)), pl.BlockSpec((COLS, FEAT), lambda j: (j, 0)),
            whole(GROUP, FEAT), whole(GROUP, FEAT),
        ],
        compiler_params=pltpu.CompilerParams(vmem_limit_bytes=60 << 20),
        cost_estimate=pl.CostEstimate(flops=10 << 30, bytes_accessed=25 << 20, transcendentals=0),
    )(xt, g, at, hg, mask_in, mask_out, output, input_grad)


def body(inputs, cotangent, w_in, w_out, mask_in, mask_out):
    mask_out = mask_out.T
    made = run_pipeline(inputs, cotangent, w_in, w_out, mask_in, mask_out)
    w_in_grad, w_out_grad, output, input_grad = run_weight_grads(*made, mask_in, mask_out)
    return (output, input_grad, w_in_grad, w_out_grad)


def solution(mesh):
    in_specs = (
        P(("row", "col"), None),
        P("row", "col"),
        P("col", "row"),
        P("row", "col"),
        P("col", "row"),
        P("row", "col"),
    )
    out_specs = (P("row", "col"), P("row", "col"), P("col", "row"), P("row", "col"))
    return jax.shard_map(body, mesh=mesh, in_specs=in_specs, out_specs=out_specs, check_vma=False)
```

```python
import functools

import jax
import jax.numpy as jnp
from jax import lax
from jax.experimental import pallas as pl
from jax.experimental.pallas import tpu as pltpu
from jax.sharding import PartitionSpec as P

MESH = pl.DeviceIdType.MESH
F32 = jnp.float32
BF16 = jnp.bfloat16

GROUP = 128
GROUPS = 8
UNITS = 2 * GROUPS
FEAT = 768
COLS = 768
RANGES = (((0, 128), (0, 1, 2)), ((128, 256), (0, 2, 1)), ((256, 512), (1, 2, 0)), ((512, 768), (2, 1, 0)))
TILE = 256
NT = (((1,), (1,)), ((), ()))
TN = (((0,), (0,)), ((), ()))


def flip(position, by):
    return (position % 2 + by % 2) % 2 + 2 * ((position // 2 + by // 2) % 2)


def one_hot(shape, along, shift, offset):
    wide = lax.broadcasted_iota(jnp.int32, shape, along)
    other = lax.broadcasted_iota(jnp.int32, shape, 1 - along)
    return (lax.shift_right_logical(wide, shift) + offset == other).astype(F32).astype(BF16)


def gelu_parts(hidden, act_grad):
    c = 0.7978845608028654
    square = hidden * hidden
    inner = jnp.tanh(c * hidden * (1.0 + 0.044715 * square))
    cdf = 0.5 * (1.0 + inner)
    slope = cdf + 0.5 * hidden * (1.0 - inner * inner) * (c * (1.0 + 0.134145 * square))
    return hidden * cdf, act_grad * slope


def pipeline(
    inputs_ref, cot_ref, w_in_ref, w_out_ref, mask_in_ref, mask_out_ref,
    out_ref, ig_ref, xt_out, g_out, at_out, hg_out,
    w1, w2, s1, s2, m_in, m_out, a2a_send, a2a_recv, xg, part, part_send,
    half, half_send, quarter, quarter_send, half_recv, quarter_recv, eighth_recv, ahg, prod, sib_send, sib_recv,
    row_send, row_recv, row_own, hop_send, hop_recv, at_buf, hg_buf, xt_buf,
    load_sem, wsend_sem, wrecv_sem, a_ssem, a_rsem, g_ssem, g_rsem, f_ssem, f_rsem,
    sum_ss, sum_rs, gather_ss, gather_rs,
    sib_ss, sib_rs, row_ss, row_rs, keep_sem, give_ss, give_rs, store_sem, hop_ss, hop_rs,
):
    row, col = lax.axis_index("row"), lax.axis_index("col")
    z, xh = row // 2, row % 2
    chip, core = col // 2, col % 2
    y, x = chip // 2, chip % 2

    sibling = (row, chip * 2 + 1 - core)
    x_mate = (row, (y * 2 + 1 - x) * 2 + core)
    mate = [x_mate] + [(row, (flip(y, d) * 2 + x) * 2 + core) for d in (1, 3)]
    bit = [x, (y // 2 + y % 2) % 2, y // 2]
    hop_mate = (z * 2 + 1 - xh, col)
    z_mate = [(flip(z, d) * 2 + xh, col) for d in (1, 2, 3)]
    col_mate = [(row, (col + d) % 16) for d in range(1, 16)]
    near = z * 2 + 1 - xh
    near_mate = [(near, (col + d) % 16) for d in range(1, 16)]

    def remote(source, target, send, recv, device):
        return pltpu.make_async_remote_copy(
            src_ref=source, dst_ref=target, send_sem=send, recv_sem=recv,
            device_id=device, device_id_type=MESH,
        )

    def part_of(base, u):
        return pl.ds(pl.multiple_of(base * 2 * COLS + u * COLS, COLS), COLS)

    loads = []
    for u in (0, 1):
        loads += [
            (w_out_ref.at[part_of(1 - core, u), :], s2.at[u]),
            (w_in_ref.at[:, part_of(1 - core, u)], s1.at[u]),
            (w_out_ref.at[part_of(core, u), :], w2.at[0, u]),
            (w_in_ref.at[:, part_of(core, u)], w1.at[0, u]),
        ]
    loads.append((cot_ref, xg.at[0, GROUPS - 1, 1]))
    loads = [pltpu.make_async_copy(*pair, load_sem.at[i]) for i, pair in enumerate(loads)]
    for load in loads:
        load.start()

    barrier = pltpu.get_barrier_semaphore()
    for device in [*col_mate, *near_mate, hop_mate, *z_mate]:
        pl.semaphore_signal(barrier, inc=1, device_id=device, device_id_type=MESH)

    for c in range(16):
        block = inputs_ref[:, c * FEAT : (c + 1) * FEAT].astype(F32)
        a2a_send[c] = jnp.concatenate([block[:, : FEAT // 2], block[:, FEAT // 2 :]], axis=0).astype(BF16)
    pl.semaphore_wait(barrier, 34)

    def a2a_copy(d, other):
        to = (col + d) % 16
        device = (near if other else row, to)
        return remote(a2a_send.at[to], a2a_recv.at[other, col], a_ssem.at[other, d], a_rsem.at[other, d], device)

    a2a_copies = [a2a_copy(d, 1) for d in range(16)] + [a2a_copy(d, 0) for d in range(1, 16)]
    for copy in a2a_copies:
        copy.start()
    a2a_recv[0, col] = a2a_send[col]

    def group_copy(source, target, k, device):
        return remote(xg.at[0, source, k], xg.at[0, target, k], g_ssem.at[target, k], g_rsem.at[target, k], device)

    def forward(s):
        return remote(xg.at[0, s], xg.at[1, s], f_ssem.at[s], f_rsem.at[s], sibling)

    mask_in = mask_in_ref[...].astype(F32).astype(BF16)
    m_in[0] = jnp.dot(mask_in, one_hot((48, 2 * COLS), 1, 6, core * 24), preferred_element_type=F32)
    m_in[1] = jnp.dot(mask_in, one_hot((48, 2 * COLS), 1, 6, (1 - core) * 24), preferred_element_type=F32)
    mask_out = mask_out_ref[...].astype(F32).astype(BF16)
    m_out[...] = lax.dot_general(mask_out, one_hot((12, FEAT), 1, 6, 0), TN, preferred_element_type=F32)

    def mask_rows(weight, masks, first, columns):
        def step(i, carry):
            here = pl.ds(pl.multiple_of(i * 64, 64), 64)
            keep = jnp.broadcast_to(masks[pl.ds(first + i, 1), columns], (64, COLS)).astype(BF16)
            weight[here, :] = weight[here, :] * keep
            return carry

        lax.fori_loop(0, 12, step, 0)

    gives = []
    loads[8].wait()
    group_copy(7, 0, 1, hop_mate).start()
    for u in (0, 1):
        columns = slice(u * COLS, (u + 1) * COLS)
        loads[4 * u].wait()
        mask_rows(s2.at[u], m_out, (1 - core) * 24 + u * 12, slice(None))
        gives.append(remote(s2.at[u], w2.at[1, u], wsend_sem.at[2 * u], wrecv_sem.at[2 * u], sibling))
        gives[-1].start()
        loads[4 * u + 1].wait()
        mask_rows(s1.at[u], m_in.at[1], 0, columns)
        gives.append(remote(s1.at[u], w1.at[1, u], wsend_sem.at[2 * u + 1], wrecv_sem.at[2 * u + 1], sibling))
        gives[-1].start()

    for copy in a2a_copies:
        copy.wait_recv()
    for other, s in ((1, 0), (0, 7)):
        for pair in range(8):
            rows = []
            for c in (2 * pair, 2 * pair + 1):
                block = a2a_recv[other, c].astype(F32)
                rows.append(jnp.concatenate([block[:8], block[8:]], axis=1))
            xg[0, s, 0, pair * 16 : (pair + 1) * 16, :] = jnp.concatenate(rows, axis=0).astype(BF16)
        if other:
            group_copy(7, 0, 1, hop_mate).wait_recv()
            forward(0).start()
            for k in (0, 1):
                group_copy(0, 1, k, z_mate[0]).start()

    for u in (0, 1):
        loads[4 * u + 2].wait()
        mask_rows(w2.at[0, u], m_out, core * 24 + u * 12, slice(None))
        loads[4 * u + 3].wait()
        mask_rows(w1.at[0, u], m_in.at[0], 0, slice(u * COLS, (u + 1) * COLS))

    for give in gives[:2]:
        give.wait_recv()

    def choose(order, done, axis=None, own=True):
        where = [slice(None)] * 3
        if axis is not None:
            where[axis] = bit[axis] if own else 1 - bit[axis]
        return tuple(where[d] for d in range(3) if d not in order[:done])

    def sum_copies(n, stage):
        two, copies = n % 2, []
        source = (part_send, half_send, quarter_send)[stage]
        target = (half_recv, quarter_recv, eighth_recv)[stage]
        for i, ((low, high), order) in enumerate(RANGES):
            axis = order[stage]
            copies.append(
                remote(
                    source.at[(two, slice(None), *choose(order, stage, axis, False), slice(None), slice(low, high))],
                    target.at[n, ..., low:high],
                    sum_ss.at[stage, two, i], sum_rs.at[stage, n, i], mate[axis],
                )
            )
        return copies

    def gather_copies(n, stage):
        two, copies = n % 2, []
        for i, ((low, high), order) in enumerate(RANGES):
            where = tuple(bit[d] if d in order[: stage + 1] else slice(None) for d in range(3))
            block = ahg.at[(n, slice(None), *where, slice(None), slice(low, high))]
            copies.append(remote(block, block, gather_ss.at[stage, two, i], gather_rs.at[stage, n, i], mate[order[stage]]))
        return copies

    def received(n, stage, own):
        two = n % 2
        for copy in sum_copies(n, stage):
            copy.wait()
        arrived = (half_recv, quarter_recv, eighth_recv)[stage]
        for (low, high), order in RANGES:
            here = own[(two, slice(None), *choose(order, stage, order[stage]), slice(None), slice(low, high))]
            yield low, high, here + arrived[n, ..., low:high].astype(F32)

    def sib_copy(s):
        two = s % 2
        return remote(sib_send.at[two], sib_recv.at[s], sib_ss.at[two], sib_rs.at[s], sibling)

    def tokens_of(s):
        return pl.ds(pl.multiple_of(s * GROUP, GROUP), GROUP)

    def keep_copies(n):
        s, u, two = n // 2, n % 2, n % 2
        pairs = [(at_buf.at[two], at_out.at[core, u, :, tokens_of(s)]), (hg_buf.at[two], hg_out.at[core, u, tokens_of(s), :])]
        copies = []
        for k, (source, target) in enumerate(pairs):
            copies.append(pltpu.make_async_copy(source, target, keep_sem.at[two, k]))
            copies.append(remote(source, target, give_ss.at[two, k], give_rs.at[n, k], sibling))
        return copies

    def store_copies(s):
        return [
            pltpu.make_async_copy(xt_buf, xt_out.at[:, tokens_of(s)], store_sem.at[0]),
            pltpu.make_async_copy(xg.at[0, s, 1], g_out.at[tokens_of(s), :], store_sem.at[1]),
        ]

    def row_copy(s):
        two = s % 2
        by = jnp.where(s < 4, s, s - 3)
        return remote(row_send.at[two], row_recv.at[s], row_ss.at[two], row_rs.at[s], (flip(z, by) * 2 + xh, col))

    def multiply(n):
        s, u, two = n // 2, n % 2, n % 2

        @pl.when(u == 0)
        def _():
            forward(s).wait_recv()

        @pl.when(n == 1)
        def _():
            for give in gives[2:]:
                give.wait_recv()

        for j in range(COLS // TILE):
            here = slice(j * TILE, (j + 1) * TILE)
            total = lax.dot_general(xg[0, s, 1], w2[0, u, here, :], NT, preferred_element_type=F32)
            total += lax.dot_general(xg[1, s, 1], w2[1, u, here, :], NT, preferred_element_type=F32)
            total = total.reshape(2, 2, 2, 16, TILE)
            part[two, 1, ..., here] = total
            part_send[two, 1, ..., here] = total.astype(BF16)
        for j in range(COLS // TILE):
            here = slice(j * TILE, (j + 1) * TILE)
            total = jnp.dot(xg[0, s, 0], w1[0, u, :, here], preferred_element_type=F32)
            total += jnp.dot(xg[1, s, 0], w1[1, u, :, here], preferred_element_type=F32)
            total = total.reshape(2, 2, 2, 16, TILE)
            part[two, 0, ..., here] = total
            part_send[two, 0, ..., here] = total.astype(BF16)
        for copy in sum_copies(n, 0):
            copy.start()

    def receive(s):
        @pl.when(s < GROUPS - 1)
        def _():
            for k in (0, 1):
                group_copy(7, s, k, hop_mate).wait_recv()

        forward(s).start()

    def relay(t):
        for at, source, target, d in ((0, 0, 2, 2), (2, 0, 3, 3), (3, 7, 4, 1), (5, 7, 5, 2), (7, 7, 6, 3)):

            @pl.when(t == at)
            def _(source=source, target=target, d=d):
                for k in (0, 1):
                    group_copy(source, target, k, z_mate[d - 1]).start()

    def add_half(n):
        for low, high, total in received(n, 0, part):
            half[n % 2, ..., low:high] = total
            half_send[n % 2, ..., low:high] = total.astype(BF16)
        for copy in sum_copies(n, 1):
            copy.start()

    def add_quarter(n):
        for low, high, total in received(n, 1, half):
            quarter[n % 2, ..., low:high] = total
            quarter_send[n % 2, ..., low:high] = total.astype(BF16)
        for copy in sum_copies(n, 2):
            copy.start()

    def activate(n):
        for low, high, total in received(n, 2, quarter):
            for k, values in enumerate(gelu_parts(total[0], total[1])):
                ahg[n, k, bit[0], bit[1], bit[2], :, low:high] = values.astype(BF16)
        for copy in gather_copies(n, 2):
            copy.start()

    def spread(n, stage):
        for copy in gather_copies(n, stage + 1):
            copy.wait()
        for copy in gather_copies(n, stage):
            copy.start()

    def project(n):
        s, u, two = n // 2, n % 2, (n // 2) % 2
        for copy in gather_copies(n, 0):
            copy.wait()
        hg_buf[n % 2] = ahg[n, 1].reshape(GROUP, COLS)

        def products(fc, here):
            activated, hidden_grad = (ahg[n, k].reshape(GROUP, COLS) for k in (0, 1))
            return (
                jnp.dot(activated, w2[fc, u, :, here], preferred_element_type=F32),
                lax.dot_general(hidden_grad, w1[fc, u, here, :], NT, preferred_element_type=F32),
            )

        @pl.when(u == 0)
        def _():
            for fc in (1, 0):
                for j in range(FEAT // TILE):
                    here = slice(j * TILE, (j + 1) * TILE)
                    for k, value in enumerate(products(fc, here)):
                        prod[two, fc, k, :, here] = value

        @pl.when(u == 1)
        def _():
            for j in range(FEAT // TILE):
                here = slice(j * TILE, (j + 1) * TILE)
                for k, value in enumerate(products(1, here)):
                    sib_send[two, k, :, here] = (prod[two, 1, k, :, here] + value).astype(BF16)
            sib_copy(s).start()
            for j in range(FEAT // TILE):
                here = slice(j * TILE, (j + 1) * TILE)
                for k, value in enumerate(products(0, here)):
                    prod[two, 0, k, :, here] += value

        at_buf[n % 2] = ahg[n, 0].reshape(GROUP, COLS).T
        for copy in keep_copies(n):
            copy.start()

        @pl.when(u == 0)
        def _():
            xt_buf[...] = xg[0, s, 0].T
            for copy in store_copies(s):
                copy.start()

    def hand_on(n):
        s, two = n // 2, (n // 2) % 2

        @pl.when(n % 2 == 1)
        def _():
            sib_copy(s).wait()

            @pl.when(jnp.logical_or(s == 0, s == 7))
            def _():
                row_own[jnp.where(s == 0, 1, 0)] = prod[two, 0] + sib_recv[s].astype(F32)

            @pl.when(jnp.logical_and(s != 0, s != 7))
            def _():
                row_send[two] = (prod[two, 0] + sib_recv[s].astype(F32)).astype(BF16)
                row_copy(s).start()

    def finish(n):
        s = n // 2
        for copy in keep_copies(n):
            copy.wait()

        @pl.when(n % 2 == 0)
        def _():
            for copy in store_copies(s):
                copy.wait()

    def settle(n):
        s = n // 2

        @pl.when(jnp.logical_and(n % 2 == 1, jnp.logical_and(s != 0, s != 7)))
        def _():
            row_copy(s).wait_send()

    def hop_copy(k, i):
        rows = slice(i * 32, (i + 1) * 32)
        return remote(hop_send.at[k, rows], hop_recv.at[k, rows], hop_ss.at[k, i], hop_rs.at[k, i], hop_mate)

    def step(t, carry):
        def at(lag, stage):
            pl.when(jnp.logical_and(t >= lag, t < UNITS + lag))(lambda: stage(t - lag))

        at(0, multiply)
        at(1, add_half)
        at(2, add_quarter)
        at(3, activate)
        at(4, lambda n: spread(n, 1))
        at(5, lambda n: spread(n, 0))

        pl.when(t < 8)(lambda: relay(t))

        @pl.when(jnp.logical_and(t % 2 == 1, t < UNITS - 2))
        def _():
            receive(t // 2 + 1)

        at(7, finish)
        at(6, project)
        at(9, settle)
        at(7, hand_on)

        @pl.when(t == 16)
        def _():
            total = row_own[1]
            for s in (1, 2, 3):
                row_copy(s).wait_recv()
                total += row_recv[s].astype(F32)
            hop_send[...] = total.astype(BF16)

        for i in range(4):

            @pl.when(t == 16 + i)
            def _(i=i):
                for k in (0, 1):
                    hop_copy(k, i).start()

        return carry

    lax.fori_loop(0, UNITS + 7, step, 0)

    total = row_own[0]
    for s in (4, 5, 6):
        row_copy(s).wait_recv()
        total += row_recv[s].astype(F32)
    for i in range(4):
        for k in (0, 1):
            hop_copy(k, i).wait()
    total += hop_recv[...].astype(F32)
    out_ref[...] = total[0].astype(BF16)
    ig_ref[...] = total[1].astype(BF16)

    for give in gives:
        give.wait_send()
    for copy in a2a_copies:
        copy.wait_send()
    for s in range(GROUPS):
        forward(s).wait_send()
    for s in range(GROUPS - 1):
        for k in (0, 1):
            if s or k:
                group_copy(7, s, k, hop_mate).wait_send()


def run_pipeline(inputs, cotangent, w_in, w_out, mask_in, mask_out):
    vmem = pl.BlockSpec(memory_space=pltpu.VMEM)
    hbm = pl.BlockSpec(memory_space=pltpu.HBM)
    dma = pltpu.SemaphoreType.DMA
    tokens = GROUP * GROUPS
    return pl.pallas_call(
        pipeline,
        out_shape=[
            jax.ShapeDtypeStruct((GROUP, FEAT), BF16),
            jax.ShapeDtypeStruct((GROUP, FEAT), BF16),
            jax.ShapeDtypeStruct((FEAT, tokens), BF16),
            jax.ShapeDtypeStruct((tokens, FEAT), BF16),
            jax.ShapeDtypeStruct((2, 2, COLS, tokens), BF16),
            jax.ShapeDtypeStruct((2, 2, tokens, COLS), BF16),
        ],
        in_specs=[vmem, hbm, hbm, hbm, vmem, vmem],
        out_specs=[vmem, vmem, hbm, hbm, hbm, hbm],
        scratch_shapes=[
            pltpu.VMEM((2, 2, FEAT, COLS), BF16),
            pltpu.VMEM((2, 2, COLS, FEAT), BF16),
            pltpu.VMEM((2, FEAT, COLS), BF16),
            pltpu.VMEM((2, COLS, FEAT), BF16),
            pltpu.VMEM((2, 12, 2 * COLS), F32),
            pltpu.VMEM((48, FEAT), F32),
            pltpu.VMEM((16, 16, FEAT // 2), BF16),
            pltpu.VMEM((2, 16, 16, FEAT // 2), BF16),
            pltpu.VMEM((2, GROUPS, 2, GROUP, FEAT), BF16),
            pltpu.VMEM((2, 2, 2, 2, 2, 16, COLS), F32),
            pltpu.VMEM((2, 2, 2, 2, 2, 16, COLS), BF16),
            pltpu.VMEM((2, 2, 2, 2, 16, COLS), F32),
            pltpu.VMEM((2, 2, 2, 2, 16, COLS), BF16),
            pltpu.VMEM((2, 2, 2, 16, COLS), F32),
            pltpu.VMEM((2, 2, 2, 16, COLS), BF16),
            pltpu.VMEM((UNITS, 2, 2, 2, 16, COLS), BF16),
            pltpu.VMEM((UNITS, 2, 2, 16, COLS), BF16),
            pltpu.VMEM((UNITS, 2, 16, COLS), BF16),
            pltpu.VMEM((UNITS, 2, 2, 2, 2, 16, COLS), BF16),
            pltpu.VMEM((2, 2, 2, GROUP, FEAT), F32),
            pltpu.VMEM((2, 2, GROUP, FEAT), BF16),
            pltpu.VMEM((GROUPS, 2, GROUP, FEAT), BF16),
            pltpu.VMEM((2, 2, GROUP, FEAT), BF16),
            pltpu.VMEM((GROUPS, 2, GROUP, FEAT), BF16),
            pltpu.VMEM((2, 2, GROUP, FEAT), F32),
            pltpu.VMEM((2, GROUP, FEAT), BF16),
            pltpu.VMEM((2, GROUP, FEAT), BF16),
            pltpu.VMEM((2, COLS, GROUP), BF16),
            pltpu.VMEM((2, GROUP, COLS), BF16),
            pltpu.VMEM((FEAT, GROUP), BF16),
            dma((9,)), dma((4,)), dma((4,)),
            dma((2, 16)), dma((2, 16)),
            dma((GROUPS, 2)), dma((GROUPS, 2)), dma((GROUPS,)), dma((GROUPS,)),
            dma((3, 2, 4)), dma((3, UNITS, 4)), dma((3, 2, 4)), dma((3, UNITS, 4)),
            dma((2,)), dma((GROUPS,)), dma((2,)), dma((GROUPS,)),
            dma((2, 2)), dma((2, 2)), dma((UNITS, 2)), dma((2,)),
            dma((2, 4)), dma((2, 4)),
        ],
        compiler_params=pltpu.CompilerParams(
            collective_id=1, has_side_effects=True, vmem_limit_bytes=60 << 20
        ),
        cost_estimate=pl.CostEstimate(flops=20 << 30, bytes_accessed=30 << 20, transcendentals=1 << 20),
    )(inputs, cotangent, w_in, w_out, mask_in, mask_out)


def weight_grads(
    xt_ref, g_ref, at_ref, hg_ref, mask_in_ref, mask_out_ref, out_in, ig_in, w_in_ref, w_out_ref, out_ref, ig_ref
):
    j = pl.program_id(0)

    @pl.when(j == 0)
    def _():
        out_ref[...] = out_in[...]
        ig_ref[...] = ig_in[...]

    mask = mask_in_ref[...].astype(F32).astype(BF16)
    keep_in = jnp.dot(mask, one_hot((48, COLS), 1, 6, j * (COLS // 64)), preferred_element_type=F32)
    mask = mask_out_ref[...].astype(F32).astype(BF16)
    rows = lax.dot_general(one_hot((12, 48), 0, 0, j * 12), mask, NT, preferred_element_type=F32).astype(BF16)
    keep_out = jnp.dot(rows, one_hot((12, FEAT), 1, 6, 0), preferred_element_type=F32)

    for left, right, keep, result in ((xt_ref, hg_ref, keep_in, w_in_ref), (at_ref, g_ref, keep_out, w_out_ref)):
        for r in range(FEAT // TILE):
            product = jnp.dot(left[r * TILE : (r + 1) * TILE, :], right[...], preferred_element_type=F32)
            for i in range(TILE // 64):
                b = r * (TILE // 64) + i
                value = product[i * 64 : (i + 1) * 64, :] * keep[b : b + 1, :]
                result[b * 64 : (b + 1) * 64, :] = value.astype(BF16)


def run_weight_grads(output, input_grad, xt, g, at, hg, mask_in, mask_out):
    tokens = GROUP * GROUPS

    def whole(*shape):
        return pl.BlockSpec(shape, lambda j: (0, 0))

    def tile(*shape):
        return pl.BlockSpec((None, None, *shape), lambda j: (j // 2, j % 2, 0, 0))

    return pl.pallas_call(
        weight_grads,
        grid=(4,),
        out_shape=[
            jax.ShapeDtypeStruct((FEAT, 4 * COLS), BF16),
            jax.ShapeDtypeStruct((4 * COLS, FEAT), BF16),
            jax.ShapeDtypeStruct((GROUP, FEAT), BF16),
            jax.ShapeDtypeStruct((GROUP, FEAT), BF16),
        ],
        in_specs=[
            whole(FEAT, tokens), whole(tokens, FEAT), tile(COLS, tokens), tile(tokens, COLS),
            whole(12, 48), whole(12, 48), whole(GROUP, FEAT), whole(GROUP, FEAT),
        ],
        out_specs=[
            pl.BlockSpec((FEAT, COLS), lambda j: (0, j)), pl.BlockSpec((COLS, FEAT), lambda j: (j, 0)),
            whole(GROUP, FEAT), whole(GROUP, FEAT),
        ],
        compiler_params=pltpu.CompilerParams(vmem_limit_bytes=60 << 20),
        cost_estimate=pl.CostEstimate(flops=10 << 30, bytes_accessed=25 << 20, transcendentals=0),
    )(xt, g, at, hg, mask_in, mask_out, output, input_grad)


def body(inputs, cotangent, w_in, w_out, mask_in, mask_out):
    mask_out = mask_out.T
    made = run_pipeline(inputs, cotangent, w_in, w_out, mask_in, mask_out)
    w_in_grad, w_out_grad, output, input_grad = run_weight_grads(*made, mask_in, mask_out)
    return (output, input_grad, w_in_grad, w_out_grad)


def solution(mesh):
    in_specs = (
        P(("row", "col"), None),
        P("row", "col"),
        P("col", "row"),
        P("row", "col"),
        P("col", "row"),
        P("row", "col"),
    )
    out_specs = (P("row", "col"), P("row", "col"), P("col", "row"), P("row", "col"))
    return jax.shard_map(body, mesh=mesh, in_specs=in_specs, out_specs=out_specs, check_vma=False)
```

```python
import functools

import jax
import jax.numpy as jnp
from jax import lax
from jax.experimental import pallas as pl
from jax.experimental.pallas import tpu as pltpu
from jax.sharding import PartitionSpec as P

MESH = pl.DeviceIdType.MESH
F32 = jnp.float32
BF16 = jnp.bfloat16

GROUP = 128
GROUPS = 8
UNITS = 2 * GROUPS
FEAT = 768
COLS = 768
RANGES = (((0, 128), (0, 1, 2)), ((128, 256), (0, 2, 1)), ((256, 512), (1, 2, 0)), ((512, 768), (2, 1, 0)))
TILE = 256
NT = (((1,), (1,)), ((), ()))
TN = (((0,), (0,)), ((), ()))


def flip(position, by):
    return (position % 2 + by % 2) % 2 + 2 * ((position // 2 + by // 2) % 2)


def one_hot(shape, along, shift, offset):
    wide = lax.broadcasted_iota(jnp.int32, shape, along)
    other = lax.broadcasted_iota(jnp.int32, shape, 1 - along)
    return (lax.shift_right_logical(wide, shift) + offset == other).astype(F32).astype(BF16)


def gelu_parts(hidden, act_grad):
    c = 0.7978845608028654
    square = hidden * hidden
    inner = jnp.tanh(c * hidden * (1.0 + 0.044715 * square))
    cdf = 0.5 * (1.0 + inner)
    slope = cdf + 0.5 * hidden * (1.0 - inner * inner) * (c * (1.0 + 0.134145 * square))
    return hidden * cdf, act_grad * slope


def pipeline(
    inputs_ref, cot_ref, w_in_ref, w_out_ref, mask_in_ref, mask_out_ref,
    out_ref, ig_ref, xt_out, g_out, at_out, hg_out,
    w1, w2, s1, s2, m_in, m_out, a2a_send, a2a_recv, xg, part, part_send,
    half, half_send, quarter, quarter_send, half_recv, quarter_recv, eighth_recv, ahg, prod, sib_send, sib_recv,
    row_send, row_recv, row_own, hop_send, hop_recv, at_buf, hg_buf, xt_buf,
    load_sem, wsend_sem, wrecv_sem, a_ssem, a_rsem, g_ssem, g_rsem, f_ssem, f_rsem,
    sum_ss, sum_rs, gather_ss, gather_rs,
    sib_ss, sib_rs, row_ss, row_rs, keep_sem, give_ss, give_rs, store_sem, hop_ss, hop_rs,
):
    row, col = lax.axis_index("row"), lax.axis_index("col")
    z, xh = row // 2, row % 2
    chip, core = col // 2, col % 2
    y, x = chip // 2, chip % 2

    sibling = (row, chip * 2 + 1 - core)
    x_mate = (row, (y * 2 + 1 - x) * 2 + core)
    mate = [x_mate] + [(row, (flip(y, d) * 2 + x) * 2 + core) for d in (1, 3)]
    bit = [x, (y // 2 + y % 2) % 2, y // 2]
    hop_mate = (z * 2 + 1 - xh, col)
    z_mate = [(flip(z, d) * 2 + xh, col) for d in (1, 2, 3)]
    col_mate = [(row, (col + d) % 16) for d in range(1, 16)]
    near = z * 2 + 1 - xh
    near_mate = [(near, (col + d) % 16) for d in range(1, 16)]

    def remote(source, target, send, recv, device):
        return pltpu.make_async_remote_copy(
            src_ref=source, dst_ref=target, send_sem=send, recv_sem=recv,
            device_id=device, device_id_type=MESH,
        )

    def part_of(base, u):
        return pl.ds(pl.multiple_of(base * 2 * COLS + u * COLS, COLS), COLS)

    loads = []
    for u in (0, 1):
        loads += [
            (w_out_ref.at[part_of(1 - core, u), :], s2.at[u]),
            (w_in_ref.at[:, part_of(1 - core, u)], s1.at[u]),
            (w_out_ref.at[part_of(core, u), :], w2.at[0, u]),
            (w_in_ref.at[:, part_of(core, u)], w1.at[0, u]),
        ]
    loads.append((cot_ref, xg.at[0, GROUPS - 1, 1]))
    loads = [pltpu.make_async_copy(*pair, load_sem.at[i]) for i, pair in enumerate(loads)]
    for load in loads:
        load.start()

    barrier = pltpu.get_barrier_semaphore()
    for device in [*col_mate, *near_mate, hop_mate, *z_mate]:
        pl.semaphore_signal(barrier, inc=1, device_id=device, device_id_type=MESH)

    for c in range(16):
        block = inputs_ref[:, c * FEAT : (c + 1) * FEAT].astype(F32)
        a2a_send[c] = jnp.concatenate([block[:, : FEAT // 2], block[:, FEAT // 2 :]], axis=0).astype(BF16)
    pl.semaphore_wait(barrier, 34)

    def a2a_copy(d, other):
        to = (col + d) % 16
        device = (near if other else row, to)
        return remote(a2a_send.at[to], a2a_recv.at[other, col], a_ssem.at[other, d], a_rsem.at[other, d], device)

    a2a_copies = [[a2a_copy(d, other) for d in range(16) if other or d] for other in range(2)]
    for other in (1, 0):
        for copy in a2a_copies[other]:
            copy.start()
    a2a_recv[0, col] = a2a_send[col]

    def group_copy(source, target, k, device):
        return remote(xg.at[0, source, k], xg.at[0, target, k], g_ssem.at[target, k], g_rsem.at[target, k], device)

    def forward(s):
        return remote(xg.at[0, s], xg.at[1, s], f_ssem.at[s], f_rsem.at[s], sibling)

    mask_in = mask_in_ref[...].astype(F32).astype(BF16)
    m_in[0] = jnp.dot(mask_in, one_hot((48, 2 * COLS), 1, 6, core * 24), preferred_element_type=F32)
    m_in[1] = jnp.dot(mask_in, one_hot((48, 2 * COLS), 1, 6, (1 - core) * 24), preferred_element_type=F32)
    mask_out = mask_out_ref[...].astype(F32).astype(BF16)
    m_out[...] = lax.dot_general(mask_out, one_hot((12, FEAT), 1, 6, 0), TN, preferred_element_type=F32)

    def mask_rows(weight, masks, first, columns):
        def step(i, carry):
            here = pl.ds(pl.multiple_of(i * 64, 64), 64)
            keep = jnp.broadcast_to(masks[pl.ds(first + i, 1), columns], (64, COLS)).astype(BF16)
            weight[here, :] = weight[here, :] * keep
            return carry

        lax.fori_loop(0, 12, step, 0)

    gives = []
    loads[8].wait()
    group_copy(7, 0, 1, hop_mate).start()
    for u in (0, 1):
        columns = slice(u * COLS, (u + 1) * COLS)
        loads[4 * u].wait()
        mask_rows(s2.at[u], m_out, (1 - core) * 24 + u * 12, slice(None))
        gives.append(remote(s2.at[u], w2.at[1, u], wsend_sem.at[2 * u], wrecv_sem.at[2 * u], sibling))
        gives[-1].start()
        loads[4 * u + 1].wait()
        mask_rows(s1.at[u], m_in.at[1], 0, columns)
        gives.append(remote(s1.at[u], w1.at[1, u], wsend_sem.at[2 * u + 1], wrecv_sem.at[2 * u + 1], sibling))
        gives[-1].start()

    def assemble(other, s):
        for copy in a2a_copies[other]:
            copy.wait_recv()
        for pair in range(8):
            rows = []
            for c in (2 * pair, 2 * pair + 1):
                block = a2a_recv[other, c].astype(F32)
                rows.append(jnp.concatenate([block[:8], block[8:]], axis=1))
            xg[0, s, 0, pair * 16 : (pair + 1) * 16, :] = jnp.concatenate(rows, axis=0).astype(BF16)

    assemble(1, 0)
    group_copy(7, 0, 1, hop_mate).wait_recv()
    forward(0).start()
    for k in (0, 1):
        group_copy(0, 1, k, z_mate[0]).start()

    for u in (0, 1):
        loads[4 * u + 2].wait()
        mask_rows(w2.at[0, u], m_out, core * 24 + u * 12, slice(None))
        loads[4 * u + 3].wait()
        mask_rows(w1.at[0, u], m_in.at[0], 0, slice(u * COLS, (u + 1) * COLS))

    for give in gives[:2]:
        give.wait_recv()

    def choose(order, done, axis=None, own=True):
        where = [slice(None)] * 3
        if axis is not None:
            where[axis] = bit[axis] if own else 1 - bit[axis]
        return tuple(where[d] for d in range(3) if d not in order[:done])

    def sum_copies(n, stage):
        two, copies = n % 2, []
        source = (part_send, half_send, quarter_send)[stage]
        target = (half_recv, quarter_recv, eighth_recv)[stage]
        for i, ((low, high), order) in enumerate(RANGES):
            axis = order[stage]
            copies.append(
                remote(
                    source.at[(two, slice(None), *choose(order, stage, axis, False), slice(None), slice(low, high))],
                    target.at[n, ..., low:high],
                    sum_ss.at[stage, two, i], sum_rs.at[stage, n, i], mate[axis],
                )
            )
        return copies

    def gather_copies(n, stage):
        two, copies = n % 2, []
        for i, ((low, high), order) in enumerate(RANGES):
            where = tuple(bit[d] if d in order[: stage + 1] else slice(None) for d in range(3))
            block = ahg.at[(n, slice(None), *where, slice(None), slice(low, high))]
            copies.append(remote(block, block, gather_ss.at[stage, two, i], gather_rs.at[stage, n, i], mate[order[stage]]))
        return copies

    def received(n, stage, own):
        two = n % 2
        for copy in sum_copies(n, stage):
            copy.wait()
        arrived = (half_recv, quarter_recv, eighth_recv)[stage]
        for (low, high), order in RANGES:
            here = own[(two, slice(None), *choose(order, stage, order[stage]), slice(None), slice(low, high))]
            yield low, high, here + arrived[n, ..., low:high].astype(F32)

    def sib_copy(s):
        two = s % 2
        return remote(sib_send.at[two], sib_recv.at[s], sib_ss.at[two], sib_rs.at[s], sibling)

    def tokens_of(s):
        return pl.ds(pl.multiple_of(s * GROUP, GROUP), GROUP)

    def keep_copies(n):
        s, u, two = n // 2, n % 2, n % 2
        pairs = [(at_buf.at[two], at_out.at[core, u, :, tokens_of(s)]), (hg_buf.at[two], hg_out.at[core, u, tokens_of(s), :])]
        copies = []
        for k, (source, target) in enumerate(pairs):
            copies.append(pltpu.make_async_copy(source, target, keep_sem.at[two, k]))
            copies.append(remote(source, target, give_ss.at[two, k], give_rs.at[n, k], sibling))
        return copies

    def store_copies(s):
        return [
            pltpu.make_async_copy(xt_buf, xt_out.at[:, tokens_of(s)], store_sem.at[0]),
            pltpu.make_async_copy(xg.at[0, s, 1], g_out.at[tokens_of(s), :], store_sem.at[1]),
        ]

    def row_copy(s):
        two = s % 2
        by = jnp.where(s < 4, s, s - 3)
        return remote(row_send.at[two], row_recv.at[s], row_ss.at[two], row_rs.at[s], (flip(z, by) * 2 + xh, col))

    def multiply(n):
        s, u, two = n // 2, n % 2, n % 2

        @pl.when(u == 0)
        def _():
            forward(s).wait_recv()

        @pl.when(n == 1)
        def _():
            for give in gives[2:]:
                give.wait_recv()

        for j in range(COLS // TILE):
            here = slice(j * TILE, (j + 1) * TILE)
            total = lax.dot_general(xg[0, s, 1], w2[0, u, here, :], NT, preferred_element_type=F32)
            total += lax.dot_general(xg[1, s, 1], w2[1, u, here, :], NT, preferred_element_type=F32)
            total = total.reshape(2, 2, 2, 16, TILE)
            part[two, 1, ..., here] = total
            part_send[two, 1, ..., here] = total.astype(BF16)
        for j in range(COLS // TILE):
            here = slice(j * TILE, (j + 1) * TILE)
            total = jnp.dot(xg[0, s, 0], w1[0, u, :, here], preferred_element_type=F32)
            total += jnp.dot(xg[1, s, 0], w1[1, u, :, here], preferred_element_type=F32)
            total = total.reshape(2, 2, 2, 16, TILE)
            part[two, 0, ..., here] = total
            part_send[two, 0, ..., here] = total.astype(BF16)
        for copy in sum_copies(n, 0):
            copy.start()

    def receive(s):
        @pl.when(s < GROUPS - 1)
        def _():
            for k in (0, 1):
                group_copy(7, s, k, hop_mate).wait_recv()

        forward(s).start()

    def relay(t):
        pl.when(t == 0)(lambda: assemble(0, 7))

        for at, source, target, d in ((0, 0, 2, 2), (2, 0, 3, 3), (3, 7, 4, 1), (5, 7, 5, 2), (7, 7, 6, 3)):

            @pl.when(t == at)
            def _(source=source, target=target, d=d):
                for k in (0, 1):
                    group_copy(source, target, k, z_mate[d - 1]).start()

    def add_half(n):
        for low, high, total in received(n, 0, part):
            half[n % 2, ..., low:high] = total
            half_send[n % 2, ..., low:high] = total.astype(BF16)
        for copy in sum_copies(n, 1):
            copy.start()

    def add_quarter(n):
        for low, high, total in received(n, 1, half):
            quarter[n % 2, ..., low:high] = total
            quarter_send[n % 2, ..., low:high] = total.astype(BF16)
        for copy in sum_copies(n, 2):
            copy.start()

    def activate(n):
        for low, high, total in received(n, 2, quarter):
            for k, values in enumerate(gelu_parts(total[0], total[1])):
                ahg[n, k, bit[0], bit[1], bit[2], :, low:high] = values.astype(BF16)
        for copy in gather_copies(n, 2):
            copy.start()

    def spread(n, stage):
        for copy in gather_copies(n, stage + 1):
            copy.wait()
        for copy in gather_copies(n, stage):
            copy.start()

    def project(n):
        s, u, two = n // 2, n % 2, (n // 2) % 2
        for copy in gather_copies(n, 0):
            copy.wait()
        hg_buf[n % 2] = ahg[n, 1].reshape(GROUP, COLS)

        def products(fc, here):
            activated, hidden_grad = (ahg[n, k].reshape(GROUP, COLS) for k in (0, 1))
            return (
                jnp.dot(activated, w2[fc, u, :, here], preferred_element_type=F32),
                lax.dot_general(hidden_grad, w1[fc, u, here, :], NT, preferred_element_type=F32),
            )

        @pl.when(u == 0)
        def _():
            for fc in (1, 0):
                for j in range(FEAT // TILE):
                    here = slice(j * TILE, (j + 1) * TILE)
                    for k, value in enumerate(products(fc, here)):
                        prod[two, fc, k, :, here] = value

        @pl.when(u == 1)
        def _():
            for j in range(FEAT // TILE):
                here = slice(j * TILE, (j + 1) * TILE)
                for k, value in enumerate(products(1, here)):
                    sib_send[two, k, :, here] = (prod[two, 1, k, :, here] + value).astype(BF16)
            sib_copy(s).start()
            for j in range(FEAT // TILE):
                here = slice(j * TILE, (j + 1) * TILE)
                for k, value in enumerate(products(0, here)):
                    prod[two, 0, k, :, here] += value

        at_buf[n % 2] = ahg[n, 0].reshape(GROUP, COLS).T
        for copy in keep_copies(n):
            copy.start()

        @pl.when(u == 0)
        def _():
            xt_buf[...] = xg[0, s, 0].T
            for copy in store_copies(s):
                copy.start()

    def hand_on(n):
        s, two = n // 2, (n // 2) % 2

        @pl.when(n % 2 == 1)
        def _():
            sib_copy(s).wait()

            @pl.when(jnp.logical_or(s == 0, s == 7))
            def _():
                row_own[jnp.where(s == 0, 1, 0)] = prod[two, 0] + sib_recv[s].astype(F32)

            @pl.when(jnp.logical_and(s != 0, s != 7))
            def _():
                row_send[two] = (prod[two, 0] + sib_recv[s].astype(F32)).astype(BF16)
                row_copy(s).start()

    def finish(n):
        s = n // 2
        for copy in keep_copies(n):
            copy.wait()

        @pl.when(n % 2 == 0)
        def _():
            for copy in store_copies(s):
                copy.wait()

    def settle(n):
        s = n // 2

        @pl.when(jnp.logical_and(n % 2 == 1, jnp.logical_and(s != 0, s != 7)))
        def _():
            row_copy(s).wait_send()

    def hop_copy(k, i):
        rows = slice(i * 32, (i + 1) * 32)
        return remote(hop_send.at[k, rows], hop_recv.at[k, rows], hop_ss.at[k, i], hop_rs.at[k, i], hop_mate)

    def step(t, carry):
        def at(lag, stage):
            pl.when(jnp.logical_and(t >= lag, t < UNITS + lag))(lambda: stage(t - lag))

        at(0, multiply)
        at(1, add_half)
        at(2, add_quarter)
        at(3, activate)
        at(4, lambda n: spread(n, 1))
        at(5, lambda n: spread(n, 0))
        at(9, settle)
        at(7, hand_on)

        pl.when(t < 8)(lambda: relay(t))

        @pl.when(jnp.logical_and(t % 2 == 1, t < UNITS - 2))
        def _():
            receive(t // 2 + 1)

        at(7, finish)
        at(6, project)

        @pl.when(t == 16)
        def _():
            total = row_own[1]
            for s in (1, 2, 3):
                row_copy(s).wait_recv()
                total += row_recv[s].astype(F32)
            hop_send[...] = total.astype(BF16)

        for i in range(4):

            @pl.when(t == 16 + i)
            def _(i=i):
                for k in (0, 1):
                    hop_copy(k, i).start()

        return carry

    lax.fori_loop(0, UNITS + 7, step, 0)

    total = row_own[0]
    for s in (4, 5, 6):
        row_copy(s).wait_recv()
        total += row_recv[s].astype(F32)
    for i in range(4):
        for k in (0, 1):
            hop_copy(k, i).wait()
    total += hop_recv[...].astype(F32)
    out_ref[...] = total[0].astype(BF16)
    ig_ref[...] = total[1].astype(BF16)

    for give in gives:
        give.wait_send()
    for copies in a2a_copies:
        for copy in copies:
            copy.wait_send()
    for s in range(GROUPS):
        forward(s).wait_send()
    for s in range(GROUPS - 1):
        for k in (0, 1):
            if s or k:
                group_copy(7, s, k, hop_mate).wait_send()


def run_pipeline(inputs, cotangent, w_in, w_out, mask_in, mask_out):
    vmem = pl.BlockSpec(memory_space=pltpu.VMEM)
    hbm = pl.BlockSpec(memory_space=pltpu.HBM)
    dma = pltpu.SemaphoreType.DMA
    tokens = GROUP * GROUPS
    return pl.pallas_call(
        pipeline,
        out_shape=[
            jax.ShapeDtypeStruct((GROUP, FEAT), BF16),
            jax.ShapeDtypeStruct((GROUP, FEAT), BF16),
            jax.ShapeDtypeStruct((FEAT, tokens), BF16),
            jax.ShapeDtypeStruct((tokens, FEAT), BF16),
            jax.ShapeDtypeStruct((2, 2, COLS, tokens), BF16),
            jax.ShapeDtypeStruct((2, 2, tokens, COLS), BF16),
        ],
        in_specs=[vmem, hbm, hbm, hbm, vmem, vmem],
        out_specs=[vmem, vmem, hbm, hbm, hbm, hbm],
        scratch_shapes=[
            pltpu.VMEM((2, 2, FEAT, COLS), BF16),
            pltpu.VMEM((2, 2, COLS, FEAT), BF16),
            pltpu.VMEM((2, FEAT, COLS), BF16),
            pltpu.VMEM((2, COLS, FEAT), BF16),
            pltpu.VMEM((2, 12, 2 * COLS), F32),
            pltpu.VMEM((48, FEAT), F32),
            pltpu.VMEM((16, 16, FEAT // 2), BF16),
            pltpu.VMEM((2, 16, 16, FEAT // 2), BF16),
            pltpu.VMEM((2, GROUPS, 2, GROUP, FEAT), BF16),
            pltpu.VMEM((2, 2, 2, 2, 2, 16, COLS), F32),
            pltpu.VMEM((2, 2, 2, 2, 2, 16, COLS), BF16),
            pltpu.VMEM((2, 2, 2, 2, 16, COLS), F32),
            pltpu.VMEM((2, 2, 2, 2, 16, COLS), BF16),
            pltpu.VMEM((2, 2, 2, 16, COLS), F32),
            pltpu.VMEM((2, 2, 2, 16, COLS), BF16),
            pltpu.VMEM((UNITS, 2, 2, 2, 16, COLS), BF16),
            pltpu.VMEM((UNITS, 2, 2, 16, COLS), BF16),
            pltpu.VMEM((UNITS, 2, 16, COLS), BF16),
            pltpu.VMEM((UNITS, 2, 2, 2, 2, 16, COLS), BF16),
            pltpu.VMEM((2, 2, 2, GROUP, FEAT), F32),
            pltpu.VMEM((2, 2, GROUP, FEAT), BF16),
            pltpu.VMEM((GROUPS, 2, GROUP, FEAT), BF16),
            pltpu.VMEM((2, 2, GROUP, FEAT), BF16),
            pltpu.VMEM((GROUPS, 2, GROUP, FEAT), BF16),
            pltpu.VMEM((2, 2, GROUP, FEAT), F32),
            pltpu.VMEM((2, GROUP, FEAT), BF16),
            pltpu.VMEM((2, GROUP, FEAT), BF16),
            pltpu.VMEM((2, COLS, GROUP), BF16),
            pltpu.VMEM((2, GROUP, COLS), BF16),
            pltpu.VMEM((FEAT, GROUP), BF16),
            dma((9,)), dma((4,)), dma((4,)),
            dma((2, 16)), dma((2, 16)),
            dma((GROUPS, 2)), dma((GROUPS, 2)), dma((GROUPS,)), dma((GROUPS,)),
            dma((3, 2, 4)), dma((3, UNITS, 4)), dma((3, 2, 4)), dma((3, UNITS, 4)),
            dma((2,)), dma((GROUPS,)), dma((2,)), dma((GROUPS,)),
            dma((2, 2)), dma((2, 2)), dma((UNITS, 2)), dma((2,)),
            dma((2, 4)), dma((2, 4)),
        ],
        compiler_params=pltpu.CompilerParams(
            collective_id=1, has_side_effects=True, vmem_limit_bytes=60 << 20
        ),
        cost_estimate=pl.CostEstimate(flops=20 << 30, bytes_accessed=30 << 20, transcendentals=1 << 20),
    )(inputs, cotangent, w_in, w_out, mask_in, mask_out)


def weight_grads(
    xt_ref, g_ref, at_ref, hg_ref, mask_in_ref, mask_out_ref, out_in, ig_in, w_in_ref, w_out_ref, out_ref, ig_ref
):
    j = pl.program_id(0)

    @pl.when(j == 0)
    def _():
        out_ref[...] = out_in[...]
        ig_ref[...] = ig_in[...]

    mask = mask_in_ref[...].astype(F32).astype(BF16)
    keep_in = jnp.dot(mask, one_hot((48, COLS), 1, 6, j * (COLS // 64)), preferred_element_type=F32)
    mask = mask_out_ref[...].astype(F32).astype(BF16)
    rows = lax.dot_general(one_hot((12, 48), 0, 0, j * 12), mask, NT, preferred_element_type=F32).astype(BF16)
    keep_out = jnp.dot(rows, one_hot((12, FEAT), 1, 6, 0), preferred_element_type=F32)

    for left, right, keep, result in ((xt_ref, hg_ref, keep_in, w_in_ref), (at_ref, g_ref, keep_out, w_out_ref)):
        for r in range(FEAT // TILE):
            product = jnp.dot(left[r * TILE : (r + 1) * TILE, :], right[...], preferred_element_type=F32)
            for i in range(TILE // 64):
                b = r * (TILE // 64) + i
                value = product[i * 64 : (i + 1) * 64, :] * keep[b : b + 1, :]
                result[b * 64 : (b + 1) * 64, :] = value.astype(BF16)


def run_weight_grads(output, input_grad, xt, g, at, hg, mask_in, mask_out):
    tokens = GROUP * GROUPS

    def whole(*shape):
        return pl.BlockSpec(shape, lambda j: (0, 0))

    def tile(*shape):
        return pl.BlockSpec((None, None, *shape), lambda j: (j // 2, j % 2, 0, 0))

    return pl.pallas_call(
        weight_grads,
        grid=(4,),
        out_shape=[
            jax.ShapeDtypeStruct((FEAT, 4 * COLS), BF16),
            jax.ShapeDtypeStruct((4 * COLS, FEAT), BF16),
            jax.ShapeDtypeStruct((GROUP, FEAT), BF16),
            jax.ShapeDtypeStruct((GROUP, FEAT), BF16),
        ],
        in_specs=[
            whole(FEAT, tokens), whole(tokens, FEAT), tile(COLS, tokens), tile(tokens, COLS),
            whole(12, 48), whole(12, 48), whole(GROUP, FEAT), whole(GROUP, FEAT),
        ],
        out_specs=[
            pl.BlockSpec((FEAT, COLS), lambda j: (0, j)), pl.BlockSpec((COLS, FEAT), lambda j: (j, 0)),
            whole(GROUP, FEAT), whole(GROUP, FEAT),
        ],
        compiler_params=pltpu.CompilerParams(vmem_limit_bytes=60 << 20),
        cost_estimate=pl.CostEstimate(flops=10 << 30, bytes_accessed=25 << 20, transcendentals=0),
    )(xt, g, at, hg, mask_in, mask_out, output, input_grad)


def body(inputs, cotangent, w_in, w_out, mask_in, mask_out):
    mask_out = mask_out.T
    made = run_pipeline(inputs, cotangent, w_in, w_out, mask_in, mask_out)
    w_in_grad, w_out_grad, output, input_grad = run_weight_grads(*made, mask_in, mask_out)
    return (output, input_grad, w_in_grad, w_out_grad)


def solution(mesh):
    in_specs = (
        P(("row", "col"), None),
        P("row", "col"),
        P("col", "row"),
        P("row", "col"),
        P("col", "row"),
        P("row", "col"),
    )
    out_specs = (P("row", "col"), P("row", "col"), P("col", "row"), P("row", "col"))
    return jax.shard_map(body, mesh=mesh, in_specs=in_specs, out_specs=out_specs, check_vma=False)
```

```python
import functools

import jax
import jax.numpy as jnp
from jax import lax
from jax.experimental import pallas as pl
from jax.experimental.pallas import tpu as pltpu
from jax.sharding import PartitionSpec as P

MESH = pl.DeviceIdType.MESH
F32 = jnp.float32
BF16 = jnp.bfloat16

GROUP = 128
GROUPS = 8
UNITS = 2 * GROUPS
FEAT = 768
COLS = 768
RANGES = (((0, 128), (0, 1, 2)), ((128, 256), (0, 2, 1)), ((256, 512), (1, 2, 0)), ((512, 768), (2, 1, 0)))
TILE = 256
NT = (((1,), (1,)), ((), ()))
TN = (((0,), (0,)), ((), ()))


def flip(position, by):
    return (position % 2 + by % 2) % 2 + 2 * ((position // 2 + by // 2) % 2)


def one_hot(shape, along, shift, offset):
    wide = lax.broadcasted_iota(jnp.int32, shape, along)
    other = lax.broadcasted_iota(jnp.int32, shape, 1 - along)
    return (lax.shift_right_logical(wide, shift) + offset == other).astype(F32).astype(BF16)


def gelu_parts(hidden, act_grad):
    c = 0.7978845608028654
    square = hidden * hidden
    inner = jnp.tanh(c * hidden * (1.0 + 0.044715 * square))
    cdf = 0.5 * (1.0 + inner)
    slope = cdf + 0.5 * hidden * (1.0 - inner * inner) * (c * (1.0 + 0.134145 * square))
    return hidden * cdf, act_grad * slope


def pipeline(
    inputs_ref, cot_ref, w_in_ref, w_out_ref, mask_in_ref, mask_out_ref,
    out_ref, ig_ref, xt_out, g_out, at_out, hg_out,
    w1, w2, s1, s2, m_in, m_out, a2a_send, a2a_recv, xg, part, part_send,
    half, half_send, quarter, quarter_send, half_recv, quarter_recv, eighth_recv, ahg, prod, sib_send, sib_recv,
    row_send, row_recv, row_own, hop_send, hop_recv, at_buf, hg_buf, xt_buf,
    load_sem, wsend_sem, wrecv_sem, a_ssem, a_rsem, g_ssem, g_rsem, f_ssem, f_rsem,
    sum_ss, sum_rs, gather_ss, gather_rs,
    sib_ss, sib_rs, row_ss, row_rs, keep_sem, give_ss, give_rs, store_sem, hop_ss, hop_rs,
):
    row, col = lax.axis_index("row"), lax.axis_index("col")
    z, xh = row // 2, row % 2
    chip, core = col // 2, col % 2
    y, x = chip // 2, chip % 2

    sibling = (row, chip * 2 + 1 - core)
    x_mate = (row, (y * 2 + 1 - x) * 2 + core)
    mate = [x_mate] + [(row, (flip(y, d) * 2 + x) * 2 + core) for d in (1, 3)]
    bit = [x, (y // 2 + y % 2) % 2, y // 2]
    hop_mate = (z * 2 + 1 - xh, col)
    z_mate = [(flip(z, d) * 2 + xh, col) for d in (1, 2, 3)]
    col_mate = [(row, (col + d) % 16) for d in range(1, 16)]
    near = z * 2 + 1 - xh
    near_mate = [(near, (col + d) % 16) for d in range(1, 16)]

    def remote(source, target, send, recv, device):
        return pltpu.make_async_remote_copy(
            src_ref=source, dst_ref=target, send_sem=send, recv_sem=recv,
            device_id=device, device_id_type=MESH,
        )

    def part_of(base, u):
        return pl.ds(pl.multiple_of(base * 2 * COLS + u * COLS, COLS), COLS)

    loads = []
    for u in (0, 1):
        loads += [
            (w_out_ref.at[part_of(1 - core, u), :], s2.at[u]),
            (w_in_ref.at[:, part_of(1 - core, u)], s1.at[u]),
            (w_out_ref.at[part_of(core, u), :], w2.at[0, u]),
            (w_in_ref.at[:, part_of(core, u)], w1.at[0, u]),
        ]
    loads.append((cot_ref, xg.at[0, GROUPS - 1, 1]))
    loads = [pltpu.make_async_copy(*pair, load_sem.at[i]) for i, pair in enumerate(loads)]
    for load in loads:
        load.start()

    barrier = pltpu.get_barrier_semaphore()
    for device in [*col_mate, *near_mate, hop_mate, *z_mate]:
        pl.semaphore_signal(barrier, inc=1, device_id=device, device_id_type=MESH)

    for c in range(16):
        block = inputs_ref[:, c * FEAT : (c + 1) * FEAT].astype(F32)
        a2a_send[c] = jnp.concatenate([block[:, : FEAT // 2], block[:, FEAT // 2 :]], axis=0).astype(BF16)
    pl.semaphore_wait(barrier, 34)

    def a2a_copy(d, other):
        to = (col + d) % 16
        device = (near if other else row, to)
        return remote(a2a_send.at[to], a2a_recv.at[other, col], a_ssem.at[other, d], a_rsem.at[other, d], device)

    a2a_copies = [[a2a_copy(d, other) for d in range(16) if other or d] for other in range(2)]
    for other in (1, 0):
        for copy in a2a_copies[other]:
            copy.start()
    a2a_recv[0, col] = a2a_send[col]

    def group_copy(source, target, k, device):
        return remote(xg.at[0, source, k], xg.at[0, target, k], g_ssem.at[target, k], g_rsem.at[target, k], device)

    def forward(s):
        return remote(xg.at[0, s], xg.at[1, s], f_ssem.at[s], f_rsem.at[s], sibling)

    mask_in = mask_in_ref[...].astype(F32).astype(BF16)
    m_in[0] = jnp.dot(mask_in, one_hot((48, 2 * COLS), 1, 6, core * 24), preferred_element_type=F32)
    m_in[1] = jnp.dot(mask_in, one_hot((48, 2 * COLS), 1, 6, (1 - core) * 24), preferred_element_type=F32)
    mask_out = mask_out_ref[...].astype(F32).astype(BF16)
    m_out[...] = lax.dot_general(mask_out, one_hot((12, FEAT), 1, 6, 0), TN, preferred_element_type=F32)

    def mask_rows(weight, masks, first, columns):
        def step(i, carry):
            here = pl.ds(pl.multiple_of(i * 64, 64), 64)
            keep = jnp.broadcast_to(masks[pl.ds(first + i, 1), columns], (64, COLS)).astype(BF16)
            weight[here, :] = weight[here, :] * keep
            return carry

        lax.fori_loop(0, 12, step, 0)

    gives = []
    loads[8].wait()
    group_copy(7, 0, 1, hop_mate).start()
    for u in (0, 1):
        columns = slice(u * COLS, (u + 1) * COLS)
        loads[4 * u].wait()
        mask_rows(s2.at[u], m_out, (1 - core) * 24 + u * 12, slice(None))
        gives.append(remote(s2.at[u], w2.at[1, u], wsend_sem.at[2 * u], wrecv_sem.at[2 * u], sibling))
        gives[-1].start()
        loads[4 * u + 1].wait()
        mask_rows(s1.at[u], m_in.at[1], 0, columns)
        gives.append(remote(s1.at[u], w1.at[1, u], wsend_sem.at[2 * u + 1], wrecv_sem.at[2 * u + 1], sibling))
        gives[-1].start()

    def assemble(other, s):
        for copy in a2a_copies[other]:
            copy.wait_recv()
        for pair in range(8):
            rows = []
            for c in (2 * pair, 2 * pair + 1):
                block = a2a_recv[other, c].astype(F32)
                rows.append(jnp.concatenate([block[:8], block[8:]], axis=1))
            xg[0, s, 0, pair * 16 : (pair + 1) * 16, :] = jnp.concatenate(rows, axis=0).astype(BF16)

    for u in (0, 1):
        loads[4 * u + 2].wait()
        mask_rows(w2.at[0, u], m_out, core * 24 + u * 12, slice(None))
        loads[4 * u + 3].wait()
        mask_rows(w1.at[0, u], m_in.at[0], 0, slice(u * COLS, (u + 1) * COLS))

    group_copy(7, 0, 1, hop_mate).wait_recv()
    group_copy(0, 1, 1, z_mate[0]).start()
    assemble(1, 0)
    forward(0).start()
    group_copy(0, 1, 0, z_mate[0]).start()

    for give in gives[:2]:
        give.wait_recv()

    def choose(order, done, axis=None, own=True):
        where = [slice(None)] * 3
        if axis is not None:
            where[axis] = bit[axis] if own else 1 - bit[axis]
        return tuple(where[d] for d in range(3) if d not in order[:done])

    def sum_copies(n, stage):
        two, copies = n % 2, []
        source = (part_send, half_send, quarter_send)[stage]
        target = (half_recv, quarter_recv, eighth_recv)[stage]
        for i, ((low, high), order) in enumerate(RANGES):
            axis = order[stage]
            copies.append(
                remote(
                    source.at[(two, slice(None), *choose(order, stage, axis, False), slice(None), slice(low, high))],
                    target.at[n, ..., low:high],
                    sum_ss.at[stage, two, i], sum_rs.at[stage, n, i], mate[axis],
                )
            )
        return copies

    def gather_copies(n, stage):
        two, copies = n % 2, []
        for i, ((low, high), order) in enumerate(RANGES):
            where = tuple(bit[d] if d in order[: stage + 1] else slice(None) for d in range(3))
            block = ahg.at[(n, slice(None), *where, slice(None), slice(low, high))]
            copies.append(remote(block, block, gather_ss.at[stage, two, i], gather_rs.at[stage, n, i], mate[order[stage]]))
        return copies

    def received(n, stage, own):
        two = n % 2
        for copy in sum_copies(n, stage):
            copy.wait()
        arrived = (half_recv, quarter_recv, eighth_recv)[stage]
        for (low, high), order in RANGES:
            here = own[(two, slice(None), *choose(order, stage, order[stage]), slice(None), slice(low, high))]
            yield low, high, here + arrived[n, ..., low:high].astype(F32)

    def sib_copy(s):
        two = s % 2
        return remote(sib_send.at[two], sib_recv.at[s], sib_ss.at[two], sib_rs.at[s], sibling)

    def tokens_of(s):
        return pl.ds(pl.multiple_of(s * GROUP, GROUP), GROUP)

    def keep_copies(n):
        s, u, two = n // 2, n % 2, n % 2
        pairs = [(at_buf.at[two], at_out.at[core, u, :, tokens_of(s)]), (hg_buf.at[two], hg_out.at[core, u, tokens_of(s), :])]
        copies = []
        for k, (source, target) in enumerate(pairs):
            copies.append(pltpu.make_async_copy(source, target, keep_sem.at[two, k]))
            copies.append(remote(source, target, give_ss.at[two, k], give_rs.at[n, k], sibling))
        return copies

    def store_copies(s):
        return [
            pltpu.make_async_copy(xt_buf, xt_out.at[:, tokens_of(s)], store_sem.at[0]),
            pltpu.make_async_copy(xg.at[0, s, 1], g_out.at[tokens_of(s), :], store_sem.at[1]),
        ]

    def row_copy(s):
        two = s % 2
        by = jnp.where(s < 4, s, s - 3)
        return remote(row_send.at[two], row_recv.at[s], row_ss.at[two], row_rs.at[s], (flip(z, by) * 2 + xh, col))

    def multiply(n):
        s, u, two = n // 2, n % 2, n % 2

        @pl.when(u == 0)
        def _():
            forward(s).wait_recv()

        @pl.when(n == 1)
        def _():
            for give in gives[2:]:
                give.wait_recv()

        for j in range(COLS // TILE):
            here = slice(j * TILE, (j + 1) * TILE)
            total = lax.dot_general(xg[0, s, 1], w2[0, u, here, :], NT, preferred_element_type=F32)
            total += lax.dot_general(xg[1, s, 1], w2[1, u, here, :], NT, preferred_element_type=F32)
            total = total.reshape(2, 2, 2, 16, TILE)
            part[two, 1, ..., here] = total
            part_send[two, 1, ..., here] = total.astype(BF16)
        for j in range(COLS // TILE):
            here = slice(j * TILE, (j + 1) * TILE)
            total = jnp.dot(xg[0, s, 0], w1[0, u, :, here], preferred_element_type=F32)
            total += jnp.dot(xg[1, s, 0], w1[1, u, :, here], preferred_element_type=F32)
            total = total.reshape(2, 2, 2, 16, TILE)
            part[two, 0, ..., here] = total
            part_send[two, 0, ..., here] = total.astype(BF16)
        for copy in sum_copies(n, 0):
            copy.start()

    def receive(s):
        @pl.when(s < GROUPS - 1)
        def _():
            for k in (0, 1):
                group_copy(7, s, k, hop_mate).wait_recv()

        forward(s).start()

    def relay(t):
        pl.when(t == 0)(lambda: assemble(0, 7))

        for at, source, target, d in ((0, 0, 2, 2), (2, 0, 3, 3), (3, 7, 4, 1), (5, 7, 5, 2), (7, 7, 6, 3)):

            @pl.when(t == at)
            def _(source=source, target=target, d=d):
                for k in (0, 1):
                    group_copy(source, target, k, z_mate[d - 1]).start()

    def add_half(n):
        for low, high, total in received(n, 0, part):
            half[n % 2, ..., low:high] = total
            half_send[n % 2, ..., low:high] = total.astype(BF16)
        for copy in sum_copies(n, 1):
            copy.start()

    def add_quarter(n):
        for low, high, total in received(n, 1, half):
            quarter[n % 2, ..., low:high] = total
            quarter_send[n % 2, ..., low:high] = total.astype(BF16)
        for copy in sum_copies(n, 2):
            copy.start()

    def activate(n):
        for low, high, total in received(n, 2, quarter):
            for k, values in enumerate(gelu_parts(total[0], total[1])):
                ahg[n, k, bit[0], bit[1], bit[2], :, low:high] = values.astype(BF16)
        for copy in gather_copies(n, 2):
            copy.start()

    def spread(n, stage):
        for copy in gather_copies(n, stage + 1):
            copy.wait()
        for copy in gather_copies(n, stage):
            copy.start()

    def project(n):
        s, u, two = n // 2, n % 2, (n // 2) % 2
        for copy in gather_copies(n, 0):
            copy.wait()
        hg_buf[n % 2] = ahg[n, 1].reshape(GROUP, COLS)

        def products(fc, here):
            activated, hidden_grad = (ahg[n, k].reshape(GROUP, COLS) for k in (0, 1))
            return (
                jnp.dot(activated, w2[fc, u, :, here], preferred_element_type=F32),
                lax.dot_general(hidden_grad, w1[fc, u, here, :], NT, preferred_element_type=F32),
            )

        @pl.when(u == 0)
        def _():
            for fc in (1, 0):
                for j in range(FEAT // TILE):
                    here = slice(j * TILE, (j + 1) * TILE)
                    for k, value in enumerate(products(fc, here)):
                        prod[two, fc, k, :, here] = value

        @pl.when(u == 1)
        def _():
            for j in range(FEAT // TILE):
                here = slice(j * TILE, (j + 1) * TILE)
                for k, value in enumerate(products(1, here)):
                    sib_send[two, k, :, here] = (prod[two, 1, k, :, here] + value).astype(BF16)
            sib_copy(s).start()
            for j in range(FEAT // TILE):
                here = slice(j * TILE, (j + 1) * TILE)
                for k, value in enumerate(products(0, here)):
                    prod[two, 0, k, :, here] += value

        at_buf[n % 2] = ahg[n, 0].reshape(GROUP, COLS).T
        for copy in keep_copies(n):
            copy.start()

        @pl.when(u == 0)
        def _():
            xt_buf[...] = xg[0, s, 0].T
            for copy in store_copies(s):
                copy.start()

    def hand_on(n):
        s, two = n // 2, (n // 2) % 2

        @pl.when(n % 2 == 1)
        def _():
            sib_copy(s).wait()

            @pl.when(jnp.logical_or(s == 0, s == 7))
            def _():
                row_own[jnp.where(s == 0, 1, 0)] = prod[two, 0] + sib_recv[s].astype(F32)

            @pl.when(jnp.logical_and(s != 0, s != 7))
            def _():
                row_send[two] = (prod[two, 0] + sib_recv[s].astype(F32)).astype(BF16)
                row_copy(s).start()

    def finish(n):
        s = n // 2
        for copy in keep_copies(n):
            copy.wait()

        @pl.when(n % 2 == 0)
        def _():
            for copy in store_copies(s):
                copy.wait()

    def settle(n):
        s = n // 2

        @pl.when(jnp.logical_and(n % 2 == 1, jnp.logical_and(s != 0, s != 7)))
        def _():
            row_copy(s).wait_send()

    def hop_copy(k, i):
        rows = slice(i * 32, (i + 1) * 32)
        return remote(hop_send.at[k, rows], hop_recv.at[k, rows], hop_ss.at[k, i], hop_rs.at[k, i], hop_mate)

    def step(t, carry):
        def at(lag, stage):
            pl.when(jnp.logical_and(t >= lag, t < UNITS + lag))(lambda: stage(t - lag))

        at(0, multiply)
        at(1, add_half)
        at(2, add_quarter)
        at(3, activate)
        at(4, lambda n: spread(n, 1))
        at(5, lambda n: spread(n, 0))
        at(9, settle)
        at(7, hand_on)

        pl.when(t < 8)(lambda: relay(t))

        @pl.when(jnp.logical_and(t % 2 == 1, t < UNITS - 2))
        def _():
            receive(t // 2 + 1)

        at(7, finish)
        at(6, project)

        @pl.when(t == 16)
        def _():
            total = row_own[1]
            for s in (1, 2, 3):
                row_copy(s).wait_recv()
                total += row_recv[s].astype(F32)
            hop_send[...] = total.astype(BF16)

        for i in range(4):

            @pl.when(t == 16 + i)
            def _(i=i):
                for k in (0, 1):
                    hop_copy(k, i).start()

        return carry

    lax.fori_loop(0, UNITS + 7, step, 0)

    total = row_own[0]
    for s in (4, 5, 6):
        row_copy(s).wait_recv()
        total += row_recv[s].astype(F32)
    for i in range(4):
        for k in (0, 1):
            hop_copy(k, i).wait()
    total += hop_recv[...].astype(F32)
    out_ref[...] = total[0].astype(BF16)
    ig_ref[...] = total[1].astype(BF16)

    for give in gives:
        give.wait_send()
    for copies in a2a_copies:
        for copy in copies:
            copy.wait_send()
    for s in range(GROUPS):
        forward(s).wait_send()
    for s in range(GROUPS - 1):
        for k in (0, 1):
            if s or k:
                group_copy(7, s, k, hop_mate).wait_send()


def run_pipeline(inputs, cotangent, w_in, w_out, mask_in, mask_out):
    vmem = pl.BlockSpec(memory_space=pltpu.VMEM)
    hbm = pl.BlockSpec(memory_space=pltpu.HBM)
    dma = pltpu.SemaphoreType.DMA
    tokens = GROUP * GROUPS
    return pl.pallas_call(
        pipeline,
        out_shape=[
            jax.ShapeDtypeStruct((GROUP, FEAT), BF16),
            jax.ShapeDtypeStruct((GROUP, FEAT), BF16),
            jax.ShapeDtypeStruct((FEAT, tokens), BF16),
            jax.ShapeDtypeStruct((tokens, FEAT), BF16),
            jax.ShapeDtypeStruct((2, 2, COLS, tokens), BF16),
            jax.ShapeDtypeStruct((2, 2, tokens, COLS), BF16),
        ],
        in_specs=[vmem, hbm, hbm, hbm, vmem, vmem],
        out_specs=[vmem, vmem, hbm, hbm, hbm, hbm],
        scratch_shapes=[
            pltpu.VMEM((2, 2, FEAT, COLS), BF16),
            pltpu.VMEM((2, 2, COLS, FEAT), BF16),
            pltpu.VMEM((2, FEAT, COLS), BF16),
            pltpu.VMEM((2, COLS, FEAT), BF16),
            pltpu.VMEM((2, 12, 2 * COLS), F32),
            pltpu.VMEM((48, FEAT), F32),
            pltpu.VMEM((16, 16, FEAT // 2), BF16),
            pltpu.VMEM((2, 16, 16, FEAT // 2), BF16),
            pltpu.VMEM((2, GROUPS, 2, GROUP, FEAT), BF16),
            pltpu.VMEM((2, 2, 2, 2, 2, 16, COLS), F32),
            pltpu.VMEM((2, 2, 2, 2, 2, 16, COLS), BF16),
            pltpu.VMEM((2, 2, 2, 2, 16, COLS), F32),
            pltpu.VMEM((2, 2, 2, 2, 16, COLS), BF16),
            pltpu.VMEM((2, 2, 2, 16, COLS), F32),
            pltpu.VMEM((2, 2, 2, 16, COLS), BF16),
            pltpu.VMEM((UNITS, 2, 2, 2, 16, COLS), BF16),
            pltpu.VMEM((UNITS, 2, 2, 16, COLS), BF16),
            pltpu.VMEM((UNITS, 2, 16, COLS), BF16),
            pltpu.VMEM((UNITS, 2, 2, 2, 2, 16, COLS), BF16),
            pltpu.VMEM((2, 2, 2, GROUP, FEAT), F32),
            pltpu.VMEM((2, 2, GROUP, FEAT), BF16),
            pltpu.VMEM((GROUPS, 2, GROUP, FEAT), BF16),
            pltpu.VMEM((2, 2, GROUP, FEAT), BF16),
            pltpu.VMEM((GROUPS, 2, GROUP, FEAT), BF16),
            pltpu.VMEM((2, 2, GROUP, FEAT), F32),
            pltpu.VMEM((2, GROUP, FEAT), BF16),
            pltpu.VMEM((2, GROUP, FEAT), BF16),
            pltpu.VMEM((2, COLS, GROUP), BF16),
            pltpu.VMEM((2, GROUP, COLS), BF16),
            pltpu.VMEM((FEAT, GROUP), BF16),
            dma((9,)), dma((4,)), dma((4,)),
            dma((2, 16)), dma((2, 16)),
            dma((GROUPS, 2)), dma((GROUPS, 2)), dma((GROUPS,)), dma((GROUPS,)),
            dma((3, 2, 4)), dma((3, UNITS, 4)), dma((3, 2, 4)), dma((3, UNITS, 4)),
            dma((2,)), dma((GROUPS,)), dma((2,)), dma((GROUPS,)),
            dma((2, 2)), dma((2, 2)), dma((UNITS, 2)), dma((2,)),
            dma((2, 4)), dma((2, 4)),
        ],
        compiler_params=pltpu.CompilerParams(
            collective_id=1, has_side_effects=True, vmem_limit_bytes=60 << 20
        ),
        cost_estimate=pl.CostEstimate(flops=20 << 30, bytes_accessed=30 << 20, transcendentals=1 << 20),
    )(inputs, cotangent, w_in, w_out, mask_in, mask_out)


def weight_grads(
    xt_ref, g_ref, at_ref, hg_ref, mask_in_ref, mask_out_ref, out_in, ig_in, w_in_ref, w_out_ref, out_ref, ig_ref
):
    j = pl.program_id(0)

    @pl.when(j == 0)
    def _():
        out_ref[...] = out_in[...]
        ig_ref[...] = ig_in[...]

    mask = mask_in_ref[...].astype(F32).astype(BF16)
    keep_in = jnp.dot(mask, one_hot((48, COLS), 1, 6, j * (COLS // 64)), preferred_element_type=F32)
    mask = mask_out_ref[...].astype(F32).astype(BF16)
    rows = lax.dot_general(one_hot((12, 48), 0, 0, j * 12), mask, NT, preferred_element_type=F32).astype(BF16)
    keep_out = jnp.dot(rows, one_hot((12, FEAT), 1, 6, 0), preferred_element_type=F32)

    for left, right, keep, result in ((xt_ref, hg_ref, keep_in, w_in_ref), (at_ref, g_ref, keep_out, w_out_ref)):
        for r in range(2):
            product = jnp.dot(left[r * 384 : (r + 1) * 384, :], right[...], preferred_element_type=F32)
            for i in range(6):
                b = r * 6 + i
                value = product[i * 64 : (i + 1) * 64, :] * keep[b : b + 1, :]
                result[b * 64 : (b + 1) * 64, :] = value.astype(BF16)


def run_weight_grads(output, input_grad, xt, g, at, hg, mask_in, mask_out):
    tokens = GROUP * GROUPS

    def whole(*shape):
        return pl.BlockSpec(shape, lambda j: (0, 0))

    def tile(*shape):
        return pl.BlockSpec((None, None, *shape), lambda j: (j // 2, j % 2, 0, 0))

    return pl.pallas_call(
        weight_grads,
        grid=(4,),
        out_shape=[
            jax.ShapeDtypeStruct((FEAT, 4 * COLS), BF16),
            jax.ShapeDtypeStruct((4 * COLS, FEAT), BF16),
            jax.ShapeDtypeStruct((GROUP, FEAT), BF16),
            jax.ShapeDtypeStruct((GROUP, FEAT), BF16),
        ],
        in_specs=[
            whole(FEAT, tokens), whole(tokens, FEAT), tile(COLS, tokens), tile(tokens, COLS),
            whole(12, 48), whole(12, 48), whole(GROUP, FEAT), whole(GROUP, FEAT),
        ],
        out_specs=[
            pl.BlockSpec((FEAT, COLS), lambda j: (0, j)), pl.BlockSpec((COLS, FEAT), lambda j: (j, 0)),
            whole(GROUP, FEAT), whole(GROUP, FEAT),
        ],
        compiler_params=pltpu.CompilerParams(vmem_limit_bytes=60 << 20),
        cost_estimate=pl.CostEstimate(flops=10 << 30, bytes_accessed=25 << 20, transcendentals=0),
    )(xt, g, at, hg, mask_in, mask_out, output, input_grad)


def body(inputs, cotangent, w_in, w_out, mask_in, mask_out):
    mask_out = mask_out.T
    made = run_pipeline(inputs, cotangent, w_in, w_out, mask_in, mask_out)
    w_in_grad, w_out_grad, output, input_grad = run_weight_grads(*made, mask_in, mask_out)
    return (output, input_grad, w_in_grad, w_out_grad)


def solution(mesh):
    in_specs = (
        P(("row", "col"), None),
        P("row", "col"),
        P("col", "row"),
        P("row", "col"),
        P("col", "row"),
        P("row", "col"),
    )
    out_specs = (P("row", "col"), P("row", "col"), P("col", "row"), P("row", "col"))
    return jax.shard_map(body, mesh=mesh, in_specs=in_specs, out_specs=out_specs, check_vma=False)
```
